128 devices in a mesh: ctx: 16 (over x_hi, z, core), tp: 8 (over y, x_lo).
Axes of the slice: x: 4 (x_hi: 2, x_lo: 2; x = x_hi * 2 + x_lo), y: 4, z: 4, core: 2. Of those that a mesh axis runs over, the one named last changes fastest.
Arguments:
- queries: bfloat16 [2048, 4096], P('ctx', 'tp'), may hold values from -7 to 7
- key_cache: bfloat16 [32768, 1024], P('ctx', 'tp'), may hold values from -7 to 7
- value_cache: bfloat16 [32768, 1024], P('ctx', 'tp'), may hold values from -6 to 6
- scale_exps: int32 [2, 8], P(None, 'tp'), may hold values from -1 to 1
- query_pos: int32 [2048], replicated, may hold values from 30720 to 32767, as said below
- key_pos: int32 [32768], P('ctx'), may hold values from 0 to 32767, as said below
- resid: bfloat16 [2048, 4096], P('ctx'), may hold values from -0.5 to 0.5
- out_weight: bfloat16 [4096, 4096], P('tp'), may hold values from -0.09375 to 0.09375
- norm_gain: bfloat16 [4096], replicated, may hold values from 0.5 to 1.5
- gate_weight: bfloat16 [4096, 14336], P('ctx', 'tp'), may hold values from -0.09375 to 0.09375
- up_weight: bfloat16 [4096, 14336], P('ctx', 'tp'), may hold values from -0.09375 to 0.09375
Outputs:
- activated: bfloat16 [2048, 14336], P('ctx', 'tp')
The draws below stay inside these ranges and needn't reach their ends.
Inputs may be any that keep to these rules, and one draw needn't show every extreme that they name: `key_pos`: every position 0 to 32767 stands once. `query_pos`: every position 30720 to 32767 stands once.
All inputs are finite; a program needn't handle non-finite values.
Results may differ from the reference program's by a relative error of at most 0.025.
Values may be sent and summed in bfloat16 or wider, within the bound.
A program may use at most 128 MiB of HBM per device.

```python
import math
import jax
import jax.numpy as jnp
from jax import lax

D = 4096
HEADS = 32
KV_HEADS = 8
HD = 128
FF = 14336
CACHE_DEV = 2048
QC = 2048
CTX = 32768
N_CTX = 16


def shared_draw(key):
    exponents = jax.random.randint(jax.random.fold_in(key, 50), (2, KV_HEADS), -1, 2).astype(jnp.int32)
    position_order = jax.random.permutation(jax.random.fold_in(key, 51), CTX).astype(jnp.int32)
    return (exponents, position_order)


def draw_scale_exps(key, part):
    exponents, position_order = shared_draw(key)
    return exponents


def draw_key_pos(key, part):
    exponents, position_order = shared_draw(key)
    return position_order


def draw_query_pos(key, part):
    key = jax.random.fold_in(key, 7)
    return (CTX - QC + jax.random.permutation(key, QC)).astype(jnp.int32)


def draw_key_cache(key, part):
    key = jax.random.fold_in(key, 11)
    values = jnp.clip(jax.random.normal(key, (CTX, KV_HEADS, HD), jnp.float32), -6.0, 6.0)
    return values.reshape(CTX, KV_HEADS * HD).astype(jnp.bfloat16)


def draw_queries(key, part):
    key = jax.random.fold_in(key, 13)
    values = jnp.clip(jax.random.normal(key, (QC, HEADS, HD), jnp.float32), -6.0, 6.0)
    return values.reshape(QC, HEADS * HD).astype(jnp.bfloat16)


def draw_resid(key, part):
    key = jax.random.fold_in(key, 17)
    column = jnp.arange(D, dtype=jnp.float32) / (D - 1)
    values = jnp.clip(jax.random.normal(key, (QC, D), jnp.float32), -6.0, 6.0) * 0.02 * (1.0 + 2.0 * column)[None, :]
    return values.astype(jnp.bfloat16)


def levels(own_key, dims, split, low, largest):
    def one(axis_at, shards_of):
        heights = jax.random.uniform(jax.random.fold_in(jax.random.fold_in(own_key, 6), axis_at), (shards_of,), jnp.float32, low / len(split), largest / len(split))
        return jnp.repeat(jnp.exp(heights), dims[axis_at] // shards_of).reshape((-1,) + (1,) * (len(dims) - axis_at - 1))

    level = one(*split[0])
    for cut in split[1:]:
        level = level * one(*cut)
    return level


def gaussian(stream_key, dims, scale, reach, split=(), kind=jnp.bfloat16):
    level = levels(stream_key, dims, split, -0.22, 0.18) if split else 1.0
    values = jax.random.normal(stream_key, dims, jnp.float32) * scale * level
    return jnp.minimum(jnp.maximum(values, -reach), reach).astype(kind)


def setup_inputs(seed: int = 0) -> dict:
    key_list = jax.random.split(jax.random.key(seed), 12)
    return {
        "queries": draw_queries(jax.random.fold_in(key_list[11], 71), 0),
        "key_cache": draw_key_cache(jax.random.fold_in(key_list[11], 71), 0),
        "value_cache": gaussian(key_list[2], (CTX, KV_HEADS * HD), 1.0, 6.0, ((0, 16), (1, 8))),
        "scale_exps": draw_scale_exps(jax.random.fold_in(key_list[11], 71), 0),
        "query_pos": draw_query_pos(jax.random.fold_in(key_list[11], 71), 0),
        "key_pos": draw_key_pos(jax.random.fold_in(key_list[11], 71), 0),
        "resid": draw_resid(jax.random.fold_in(key_list[11], 71), 0),
        "out_weight": gaussian(key_list[7], (HEADS * HD, D), (HEADS * HD) ** -0.5, 0.09375, ((0, 8),)),
        "norm_gain": jnp.clip(1.0 + 0.1 * jax.random.normal(key_list[8], (D,), jnp.float32), 0.5, 1.5).astype(jnp.bfloat16),
        "gate_weight": gaussian(key_list[9], (D, FF), D ** -0.5, 0.09375, ((0, 16), (1, 8))),
        "up_weight": gaussian(key_list[10], (D, FF), D ** -0.5, 0.09375, ((0, 16), (1, 8))),
    }


def reference(queries, key_cache, value_cache, scale_exps, query_pos, key_pos, resid, out_weight, norm_gain, gate_weight, up_weight):
    group_size = HEADS // KV_HEADS
    query_count = queries.shape[0]
    cache_count = key_cache.shape[0]
    query_heads = queries.reshape(query_count, KV_HEADS, group_size, HD).astype(jnp.float32)
    key_heads = key_cache.reshape(cache_count, KV_HEADS, HD)
    value_heads = value_cache.reshape(cache_count, KV_HEADS, HD)
    key_scale = jnp.exp2(scale_exps[0].astype(jnp.float32)) / math.sqrt(HD)
    value_scale = jnp.exp2(scale_exps[1].astype(jnp.float32))

    def one_head(inputs):
        query_one, key_one, value_one, key_factor, value_factor = inputs

        def visit(state, shard_index):
            out_acc, max_acc, total_acc = state
            start_row = (shard_index * CACHE_DEV).astype(jnp.int32)
            key_block = lax.dynamic_slice_in_dim(key_one, start_row, CACHE_DEV, 0).astype(jnp.float32)
            value_block = lax.dynamic_slice_in_dim(value_one, start_row, CACHE_DEV, 0).astype(jnp.float32)
            pos_block = lax.dynamic_slice_in_dim(key_pos, start_row, CACHE_DEV, 0)
            scores = jnp.einsum('qgd,kd->qgk', query_one, key_block) * key_factor
            visible = pos_block[None, None, :] <= query_pos[:, None, None]
            block_max = lax.optimization_barrier(jnp.max(jnp.where(visible, scores, -1e+30), axis=-1))
            weights = jnp.where(visible, jnp.exp(scores - block_max[..., None]), 0.0)
            block_total = lax.optimization_barrier(jnp.sum(weights, axis=-1))
            rounded = weights.astype(jnp.bfloat16).astype(jnp.float32)
            block_out = jnp.einsum('qgk,kd->qgd', rounded, value_block) * value_factor
            highest = jnp.maximum(max_acc, block_max)
            keep_old = jnp.exp(max_acc - highest)
            keep_new = jnp.exp(block_max - highest)
            out_acc = out_acc * keep_old[..., None] + block_out * keep_new[..., None]
            total_acc = total_acc * keep_old + block_total * keep_new
            return ((out_acc, highest, total_acc), None)
        start_state = (jnp.zeros((query_count, group_size, HD), jnp.float32), jnp.full((query_count, group_size), -1e+30, jnp.float32), jnp.zeros((query_count, group_size), jnp.float32))
        final_state, unused = lax.scan(visit, start_state, jnp.arange(N_CTX, dtype=jnp.int32))
        return final_state[0] / final_state[2][..., None]
    per_head = lax.map(one_head, (query_heads.transpose(1, 0, 2, 3), key_heads.transpose(1, 0, 2), value_heads.transpose(1, 0, 2), key_scale, value_scale))
    attention = per_head.transpose(1, 0, 2, 3).reshape(query_count, HEADS * HD).astype(jnp.bfloat16)
    projected = jnp.dot(attention, out_weight, preferred_element_type=jnp.float32)
    stream = resid.astype(jnp.float32) + projected
    mean_square = lax.optimization_barrier(jnp.mean(stream * stream, axis=-1, keepdims=True))
    normed = (stream * lax.rsqrt(mean_square + 1e-05) * norm_gain.astype(jnp.float32)).astype(jnp.bfloat16)
    gate = jnp.dot(normed, gate_weight, preferred_element_type=jnp.float32)
    up_part = jnp.dot(normed, up_weight, preferred_element_type=jnp.float32)
    return (jax.nn.silu(gate) * up_part).astype(jnp.bfloat16)
```

```python
import functools
import math

import jax
import jax.numpy as jnp
from jax import lax
from jax.experimental import pallas as pl
from jax.experimental.pallas import tpu as pltpu
from jax.sharding import PartitionSpec as P

HD = 128
NT = (((1,), (1,)), ((), ()))
NN = (((1,), (0,)), ((), ()))
MESH = pl.DeviceIdType.MESH
LOW = -1e30
BASE = math.log2(math.e) / math.sqrt(HD)
F32 = jnp.float32
BF16 = jnp.bfloat16
KT = 1024
CHUNKS = 7
CW = 256
EARLY = 2


def hop(r):
    low = r % 4
    return ((low * (low + 1)) // 2) % 4


def kernel(
    q_hbm,
    k_hbm,
    v_hbm,
    exps_ref,
    qp_ref,
    kp_hbm,
    resid_hbm,
    ow_hbm,
    gain_ref,
    gate_hbm,
    up_hbm,
    out_ref,
    q_all,
    kbuf,
    vbuf,
    vt,
    kpraw,
    kposb,
    sa,
    sb,
    ma,
    mb,
    acc_u,
    acc_s,
    cvec,
    usend,
    ssend,
    urecv,
    srecv,
    ow,
    resid,
    rs_send,
    rs_recv,
    sq_send,
    sq_recv,
    gsend,
    gbuf,
    wbuf,
    xsend,
    xrecv,
    pown,
    q_ss,
    q_rs,
    kv_ss,
    kv_rs,
    loc_s,
    ow_s,
    wl_s,
    u_ss,
    u_rs,
    st_ss,
    st_rs,
    d_ss,
    d_rs,
    f_ss,
    f_rs,
    r_ss,
    r_rs,
    p_ss,
    p_rs,
    sq_ss,
    sq_rs,
    g_ss,
    g_rs,
    x_ss,
    x_rs,
):
    c = lax.axis_index("ctx")
    t = lax.axis_index("tp")
    core = c % 2
    z = (c // 2) % 4
    xh = c // 8

    def ctx_at(dx, dz, dc=0):
        return ((xh + dx) % 2) * 8 + ((z + dz + 4) % 4) * 2 + (core + dc) % 2

    partner = ctx_at(0, 0, 1)
    across = ctx_at(1, 0)
    up_z = ctx_at(0, 1)
    down_z = ctx_at(0, 3)

    def remote(src, dst, ss, rs, **dev):
        return pltpu.make_async_remote_copy(
            src_ref=src, dst_ref=dst, send_sem=ss, recv_sem=rs, device_id=dev, device_id_type=MESH
        )

    lq = pltpu.make_async_copy(q_hbm, q_all.at[0], loc_s.at[0])
    lk = pltpu.make_async_copy(k_hbm, kbuf.at[1], loc_s.at[1])
    lv = pltpu.make_async_copy(v_hbm, vbuf.at[1], loc_s.at[2])
    lp = pltpu.make_async_copy(kp_hbm, kpraw.at[1], loc_s.at[3])
    for cp in (lq, lk, lv, lp):
        cp.start()

    barrier = pltpu.get_barrier_semaphore()
    peers = 0
    for r in range(1, 8):
        pl.semaphore_signal(
            barrier, inc=1, device_id={"ctx": ctx_at(r // 4, r % 4), "tp": t}, device_id_type=MESH
        )
        pl.semaphore_signal(
            barrier, inc=1, device_id={"ctx": c, "tp": (t + r) % 8}, device_id_type=MESH
        )
        pl.semaphore_signal(
            barrier, inc=1, device_id={"ctx": across, "tp": (t + r) % 8}, device_id_type=MESH
        )
        peers += 3
    pl.semaphore_signal(barrier, inc=1, device_id={"ctx": partner, "tp": t}, device_id_type=MESH)
    pl.semaphore_wait(barrier, peers + 1)

    kv = [
        remote(k_hbm, kbuf.at[0], kv_ss.at[0], kv_rs.at[0], ctx=partner, tp=t),
        remote(v_hbm, vbuf.at[0], kv_ss.at[1], kv_rs.at[1], ctx=partner, tp=t),
        remote(kp_hbm, kpraw.at[0], kv_ss.at[2], kv_rs.at[2], ctx=partner, tp=t),
    ]

    def q_copy(r):
        return remote(
            q_hbm, q_all.at[r], q_ss.at[r], q_rs.at[r], ctx=ctx_at(r // 4, 4 - hop(r)), tp=t
        )

    kv[2].start()
    for r in (1, 2, 3, 4):
        q_copy(r).start()
    kv[0].start()
    kv[1].start()

    def q_forward(r):
        return remote(q_all.at[r], q_all.at[r + 4], q_ss.at[r + 4], q_rs.at[r + 4], ctx=across, tp=t)

    own_rows = pl.multiple_of(core * 1024 + z * 256, 256)

    def own_weight(j, which):
        src = (gate_hbm, up_hbm)[which]
        return pltpu.make_async_copy(
            src.at[:, pl.ds(j * CW, CW)],
            wbuf.at[j, pl.ds(own_rows, 256), pl.ds(which * CW, CW)],
            wl_s.at[2 * j + which],
        )

    for j in range(CHUNKS):
        own_weight(j, 0).start()
        own_weight(j, 1).start()
    lres = pltpu.make_async_copy(
        resid_hbm.at[:, pl.ds(pl.multiple_of(t * 512, 512), 512)], resid, loc_s.at[4]
    )
    lres.start()

    def ow_copy(s):
        return pltpu.make_async_copy(ow_hbm.at[:, pl.ds(s * 512, 512)], ow.at[s], ow_s.at[s])

    for s in range(8):
        ow_copy(s).start()

    def block(zz):
        return pl.multiple_of(core * 1024 + ((zz + 4) % 4) * 256, 256)

    def direct(j, way):
        rows = pl.ds(own_rows, 256)
        return remote(
            wbuf.at[j, rows],
            wbuf.at[j, rows],
            d_ss.at[way, j],
            d_rs.at[way, j],
            ctx=(up_z, down_z)[way],
            tp=t,
        )

    def direct_both(j):
        direct(j, 0).start()
        direct(j, 1).start()

    def direct_arrival(j, way):
        rows = pl.ds(block(z - 1 if way == 0 else z + 1), 256)
        return remote(
            wbuf.at[j, rows], wbuf.at[j, rows], d_ss.at[way, j], d_rs.at[way, j], ctx=up_z, tp=t
        )

    def forward(j, way):
        at = wbuf.at[j, pl.ds(block(z - 1 if way == 0 else z + 1), 256), pl.ds(way * CW, CW)]
        return remote(at, at, f_ss.at[way, j], f_rs.at[way, j], ctx=(up_z, down_z)[way], tp=t)

    def forward_arrival(j, way):
        at = wbuf.at[j, pl.ds(block(z + 2), 256), pl.ds(way * CW, CW)]
        return remote(at, at, f_ss.at[way, j], f_rs.at[way, j], ctx=up_z, tp=t)

    def pass_on(j):
        for way in (0, 1):
            direct_arrival(j, way).wait_recv()
        for way in (0, 1):
            forward(j, way).start()

    def relay(j):
        at = wbuf.at[j, pl.ds(pl.multiple_of(core * 1024, 1024), 1024)]
        return remote(at, at, r_ss.at[j], r_rs.at[j], ctx=partner, tp=t)

    def relay_arrival(j):
        at = wbuf.at[j, pl.ds(pl.multiple_of((1 - core) * 1024, 1024), 1024)]
        return remote(at, at, r_ss.at[j], r_rs.at[j], ctx=partner, tp=t)

    def hand_over(j):
        for way in (0, 1):
            forward_arrival(j, way).wait_recv()
        relay(j).start()

    def prepare(half):
        def turn(a, _):
            rows = pl.ds(pl.multiple_of(a * 128, 128), 128)
            vt[half, :, rows] = jnp.transpose(vbuf[half, rows, :].astype(F32)).astype(BF16)
            places = jnp.broadcast_to(kpraw[half, pl.ds(a, 1), :].astype(F32), (128, 128))
            kposb[half, rows, :] = jnp.transpose(places)
            return 0

        lax.fori_loop(0, 16, turn, 0)

    cvec[...] = jnp.exp2(jnp.broadcast_to(exps_ref[0:1, :], (8, 128)).astype(F32)) * BASE
    acc_u[...] = jnp.zeros_like(acc_u)
    acc_s[...] = jnp.zeros_like(acc_s)
    for cp in (lq, lk, lv, lp):
        cp.wait()
    prepare(1)

    def qk(i, j, buf, mref):
        r = ((i + 1) // 2) % 8
        half = (i + 1) % 2
        owner = ctx_at(r // 4, hop(r))
        qpos = qp_ref[pl.ds(owner, 1), :].astype(F32)
        qc = jnp.concatenate([q_all[r, :, h * HD : (h + 1) * HD] for h in range(4)], axis=0)
        s = lax.dot_general(
            kbuf[half, j * KT : (j + 1) * KT], qc, NT, preferred_element_type=F32
        )
        visible = kposb[half, j * KT : (j + 1) * KT] <= qpos
        s = jnp.concatenate(
            [jnp.where(visible, s[:, h * HD : (h + 1) * HD], LOW) for h in range(4)], axis=1
        )
        buf[...] = s
        mref[...] = jnp.max(s, axis=0, keepdims=True)

    def pv(i, j, buf, mref, state):
        half = (i + 1) % 2
        factor = cvec[0:1, 0:1]
        top = jnp.maximum(state[0], mref[...])
        p = jnp.exp2((buf[...] - top) * factor)
        total = jnp.sum(p, axis=0, keepdims=True)
        out = lax.dot_general(
            vt[half, :, j * KT : (j + 1) * KT], p.astype(BF16), NN, preferred_element_type=F32
        )
        keep = jnp.exp2((state[0] - top) * factor)
        return (top, state[1] * keep + total, state[2] * keep + out)

    def u_copy(r):
        return remote(
            usend.at[r], urecv.at[r], u_ss.at[r], u_rs.at[r], ctx=ctx_at(r // 4, hop(r)), tp=t
        )

    def s_copy(r):
        return remote(
            ssend.at[r], srecv.at[r], st_ss.at[r], st_rs.at[r], ctx=ctx_at(r // 4, hop(r)), tp=t
        )

    qk(0, 0, sa, ma)

    def step(i, _):
        odd = i % 2
        r = ((i + 1) // 2) % 8
        r_next = ((i + 2) // 2) % 8

        @pl.when(i == 0)
        def _():
            for cp in kv:
                cp.wait_recv()
            prepare(0)

        @pl.when((odd == 0) & (i < 14))
        def _():
            q_copy(r_next).wait_recv()

        @pl.when((odd == 0) & (i < 6))
        def _():
            q_forward(r_next).start()

        for n in range(EARLY):

            @pl.when(i == 5 + 5 * n)
            def _(n=n):
                own_weight(n, 0).wait()
                own_weight(n, 1).wait()
                direct_both(n)

        before = jnp.where(odd == 1, LOW, acc_s[0:1, :])
        before = jnp.where(i == 0, LOW, before)
        state = (before, acc_s[1:2, :], acc_u[...])
        qk(i, 1, sb, mb)
        state = pv(i, 0, sa, ma, state)
        qk(i + 1, 0, sa, ma)
        state = pv(i, 1, sb, mb, state)
        acc_s[0:1, :] = state[0]
        acc_s[1:2, :] = state[1]
        acc_u[...] = state[2]

        @pl.when(odd == 0)
        def _():
            usend[r] = acc_u[...].astype(BF16)
            ssend[r] = acc_s[...]

        @pl.when((odd == 0) & (i > 0))
        def _():
            s_copy(r).start()
            u_copy(r).start()

        return 0

    lax.fori_loop(0, 16, step, 0)

    for j in range(EARLY, CHUNKS):
        own_weight(j, 0).wait()
        own_weight(j, 1).wait()
    direct_both(2)
    pass_on(0)
    direct_both(3)
    pass_on(1)
    for j in range(4, CHUNKS):
        direct_both(j)

    for r in range(1, 8):
        s_copy(r).wait_recv()
    tops = [acc_s[0:1, :], ssend[0, 0:1, :]] + [srecv[r, 0:1, :] for r in range(1, 8)]
    sums = [acc_s[1:2, :], ssend[0, 1:2, :]] + [srecv[r, 1:2, :] for r in range(1, 8)]
    top = functools.reduce(jnp.maximum, tops)
    factor = cvec[0:1, 0:1]
    shares = [jnp.exp2((m - top) * factor) for m in tops]
    total = functools.reduce(jnp.add, [w * l for w, l in zip(shares, sums)])
    merged = acc_u[...] * shares[0] + usend[0].astype(F32) * shares[1]
    for r in range(1, 8):
        u_copy(r).wait_recv()
        merged = merged + urecv[r].astype(F32) * shares[r + 1]
    value_factor = jnp.exp2(jnp.broadcast_to(exps_ref[1:2, :], (8, 128)).astype(F32))[0:1, 0:1]
    merged = merged * (value_factor / total)
    attention = jnp.concatenate(
        [jnp.transpose(merged[:, h * HD : (h + 1) * HD]) for h in range(4)], axis=1
    ).astype(BF16)

    for s in range(8):
        ow_copy(s).wait()

    def p_copy(k):
        return remote(
            rs_send.at[k], rs_recv.at[k], p_ss.at[k], p_rs.at[k], ctx=c, tp=(t + k) % 8
        )

    def sq_copy(k):
        return remote(
            sq_send, sq_recv.at[k], sq_ss.at[k], sq_rs.at[k], ctx=c, tp=(t + k) % 8
        )

    for k in (4, 5, 3, 2, 6, 7, 1):
        part = lax.dot_general(
            attention, ow[(t + k) % 8], NN, preferred_element_type=F32
        )
        rs_send[k] = part.astype(BF16)
        p_copy(k).start()
    stream = lax.dot_general(attention, ow[t], NN, preferred_element_type=F32)
    lres.wait()
    stream = stream + resid[...].astype(F32)
    for k in range(1, 8):
        p_copy(k).wait_recv()
        stream = stream + rs_recv[k].astype(F32)

    squares = lax.dot_general(
        jnp.ones((8, 512), F32),
        stream * stream,
        NT,
        preferred_element_type=F32,
        precision=lax.Precision.HIGHEST,
    )
    sq_send[...] = squares
    for k in range(1, 8):
        sq_copy(k).start()

    gain = gain_ref[0:1, pl.ds(pl.multiple_of(t * 512, 512), 512)].astype(F32)
    scaled = (stream * gain).astype(BF16)
    gsend[0] = scaled[:, :256]
    gsend[1] = scaled[:, 256:]
    to_half = t // 4
    lane = pl.ds(pl.multiple_of((t % 4) * 256, 256), 256)
    to_ctx = to_half * 8 + z * 2 + core
    side = (xh + to_half) % 2

    def g_copy(k):
        return remote(
            gsend,
            gbuf.at[:, side, :, lane],
            g_ss.at[k],
            g_rs.at[side * 4 + t % 4],
            ctx=to_ctx,
            tp=(t + k) % 8,
        )

    for k in (4, 3, 5, 2, 6, 1, 7):
        g_copy(k).start()

    @pl.when(side == 1)
    def _():
        g_copy(0).start()

    @pl.when(side == 0)
    def _():
        gbuf[0, 0, :, lane] = gsend[0]
        gbuf[1, 0, :, lane] = gsend[1]

    pass_on(2)
    pass_on(3)
    hand_over(0)
    hand_over(1)

    squares = sq_send[...]
    for k in range(1, 8):
        sq_copy(k).wait_recv()
        squares = squares + sq_recv[k]
    scale_row = lax.rsqrt(squares[0:1, :] * (1.0 / 4096.0) + 1e-05)
    scale = jnp.transpose(jnp.broadcast_to(scale_row, (128, 128)))[:, 0:1]

    def g_arrival(slot):
        at = gbuf.at[:, slot // 4, :, pl.ds((slot % 4) * 256, 256)]
        return remote(at, at, g_ss.at[0], g_rs.at[slot], ctx=across, tp=t)

    for slot in range(8):
        if slot < 4:

            @pl.when((to_half != xh) | (t % 4 != slot))
            def _(slot=slot):
                g_arrival(slot).wait_recv()
        else:
            g_arrival(slot).wait_recv()

    def x_copy(j):
        return remote(xsend.at[j], xrecv.at[j], x_ss.at[j], x_rs.at[j], ctx=across, tp=t)

    def finish(j):
        x_copy(j).wait_recv()
        both = (pown[j] + xrecv[j].astype(F32)) * scale
        gate = both[:, :CW]
        up = both[:, CW:]
        out_ref[:, pl.ds(pl.multiple_of(j * CW, CW), CW)] = (gate / (1.0 + jnp.exp(-gate)) * up).astype(BF16)

    def chunk(j, _):
        @pl.when(j < CHUNKS - 4)
        def _():
            pass_on(j + 4)

        relay_arrival(j).wait_recv()

        def half_product(which):
            return lax.dot_general(
                gbuf[0, which], wbuf[j, 0:1024, :], NN, preferred_element_type=F32
            ) + lax.dot_general(
                gbuf[1, which], wbuf[j, 1024:2048, :], NN, preferred_element_type=F32
            )

        xsend[j] = half_product(1).astype(BF16)
        x_copy(j).start()

        @pl.when(j < CHUNKS - 2)
        def _():
            hand_over(j + 2)

        pown[j] = half_product(0)

        @pl.when(j >= 2)
        def _():
            finish(j - 2)

        return 0

    lax.fori_loop(0, CHUNKS, chunk, 0)
    finish(CHUNKS - 2)
    finish(CHUNKS - 1)

    for cp in kv:
        cp.wait_send()
    for r in (1, 2, 3, 4):
        q_copy(r).wait_send()
    for r in (1, 2, 3):
        q_forward(r).wait_send()
    for r in range(1, 8):
        u_copy(r).wait_send()
        s_copy(r).wait_send()
        p_copy(r).wait_send()
        sq_copy(r).wait_send()
        g_copy(r).wait_send()

    @pl.when(side == 1)
    def _():
        g_copy(0).wait_send()

    for j in range(CHUNKS):
        for way in (0, 1):
            direct(j, way).wait_send()
            forward(j, way).wait_send()
        relay(j).wait_send()
        x_copy(j).wait_send()


def body(
    queries,
    key_cache,
    value_cache,
    scale_exps,
    query_pos,
    key_pos,
    resid,
    out_weight,
    norm_gain,
    gate_weight,
    up_weight,
):
    vmem = pl.BlockSpec(memory_space=pltpu.VMEM)
    hbm = pl.BlockSpec(memory_space=pl.ANY)
    V = pltpu.VMEM
    dma = pltpu.SemaphoreType.DMA
    return pl.pallas_call(
        kernel,
        out_shape=jax.ShapeDtypeStruct((128, 1792), BF16),
        in_specs=[hbm, hbm, hbm, vmem, vmem, hbm, hbm, hbm, vmem, hbm, hbm],
        out_specs=vmem,
        scratch_shapes=[
            V((8, 128, 512), BF16),
            V((2, 2048, 128), BF16),
            V((2, 2048, 128), BF16),
            V((2, 128, 2048), BF16),
            V((2, 16, 128), jnp.int32),
            V((2, 2048, 128), F32),
            V((KT, 512), F32),
            V((KT, 512), F32),
            V((1, 512), F32),
            V((1, 512), F32),
            V((128, 512), F32),
            V((8, 512), F32),
            V((8, 128), F32),
            V((8, 128, 512), BF16),
            V((8, 8, 512), F32),
            V((8, 128, 512), BF16),
            V((8, 8, 512), F32),
            V((8, 512, 512), BF16),
            V((128, 512), BF16),
            V((8, 128, 512), BF16),
            V((8, 128, 512), BF16),
            V((8, 128), F32),
            V((8, 8, 128), F32),
            V((2, 128, 256), BF16),
            V((2, 2, 128, 1024), BF16),
            V((CHUNKS, 2048, 2 * CW), BF16),
            V((CHUNKS, 128, 2 * CW), BF16),
            V((CHUNKS, 128, 2 * CW), BF16),
            V((CHUNKS, 128, 2 * CW), F32),
            dma((8,)),
            dma((8,)),
            dma((3,)),
            dma((3,)),
            dma((5,)),
            dma((8,)),
            dma((2 * CHUNKS,)),
            dma((8,)),
            dma((8,)),
            dma((8,)),
            dma((8,)),
            dma((2, CHUNKS)),
            dma((2, CHUNKS)),
            dma((2, CHUNKS)),
            dma((2, CHUNKS)),
            dma((CHUNKS,)),
            dma((CHUNKS,)),
            dma((8,)),
            dma((8,)),
            dma((8,)),
            dma((8,)),
            dma((8,)),
            dma((8,)),
            dma((CHUNKS,)),
            dma((CHUNKS,)),
        ],
        compiler_params=pltpu.CompilerParams(
            collective_id=0, has_side_effects=True, vmem_limit_bytes=60 * 2**20
        ),
        cost_estimate=pl.CostEstimate(
            flops=18_000_000_000, bytes_accessed=16_000_000, transcendentals=17_000_000
        ),
    )(
        queries,
        key_cache,
        value_cache,
        scale_exps,
        query_pos.reshape(16, 128),
        key_pos.reshape(16, 128),
        resid,
        out_weight,
        norm_gain.reshape(1, 4096),
        gate_weight,
        up_weight,
    )


def solution(mesh):
    placed = (
        P("ctx", "tp"),
        P("ctx", "tp"),
        P("ctx", "tp"),
        P(None, "tp"),
        P(),
        P("ctx"),
        P("ctx", None),
        P("tp", None),
        P(),
        P("ctx", "tp"),
        P("ctx", "tp"),
    )
    return jax.shard_map(
        body, mesh=mesh, in_specs=placed, out_specs=P("ctx", "tp"), check_vma=False
    )
```

```python
import functools
import math

import jax
import jax.numpy as jnp
from jax import lax
from jax.experimental import pallas as pl
from jax.experimental.pallas import tpu as pltpu
from jax.sharding import PartitionSpec as P

HD = 128
NT = (((1,), (1,)), ((), ()))
NN = (((1,), (0,)), ((), ()))
MESH = pl.DeviceIdType.MESH
LOW = -1e30
BASE = math.log2(math.e) / math.sqrt(HD)
F32 = jnp.float32
BF16 = jnp.bfloat16
KT = 1024
CHUNKS = 7
CW = 256
EARLY = 3


def hop(r):
    low = r % 4
    return ((low * (low + 1)) // 2) % 4


def turn_owner(n):
    n = n % 8
    late = n // 4
    return late * (4 + (n + 1) % 4) + (1 - late) * n


def kernel(
    q_hbm,
    k_hbm,
    v_hbm,
    exps_ref,
    qp_ref,
    kp_hbm,
    resid_hbm,
    ow_hbm,
    gain_hbm,
    gate_hbm,
    up_hbm,
    out_ref,
    q_all,
    kbuf,
    vbuf,
    vt,
    kpraw,
    kposb,
    sa,
    sb,
    ma,
    mb,
    acc_u,
    acc_s,
    cvec,
    usend,
    ssend,
    urecv,
    srecv,
    uhalf,
    shalf,
    ow,
    resid,
    gain_buf,
    rs_send,
    rs_recv,
    sq_send,
    sq_recv,
    sq_other,
    gsend,
    gbuf,
    wbuf,
    xsend,
    xrecv,
    pown,
    scale,
    q_ss,
    q_rs,
    kv_ss,
    kv_rs,
    loc_s,
    ow_s,
    wl_s,
    u_ss,
    u_rs,
    st_ss,
    st_rs,
    uh_rs,
    sh_rs,
    d_ss,
    d_rs,
    f_ss,
    f_rs,
    r_ss,
    r_rs,
    p_ss,
    p_rs,
    sq_ss,
    sq_rs,
    g_ss,
    g_rs,
    x_ss,
    x_rs,
):
    c = lax.axis_index("ctx")
    t = lax.axis_index("tp")
    core = c % 2
    z = (c // 2) % 4
    xh = c // 8

    def ctx_at(dx, dz, dc=0):
        return ((xh + dx) % 2) * 8 + ((z + dz + 4) % 4) * 2 + (core + dc) % 2

    partner = ctx_at(0, 0, 1)
    across = ctx_at(1, 0)
    up_z = ctx_at(0, 1)
    down_z = ctx_at(0, 3)

    def remote(src, dst, ss, rs, **dev):
        return pltpu.make_async_remote_copy(
            src_ref=src, dst_ref=dst, send_sem=ss, recv_sem=rs, device_id=dev, device_id_type=MESH
        )

    lq = pltpu.make_async_copy(q_hbm, q_all.at[0], loc_s.at[0])
    lk = pltpu.make_async_copy(k_hbm, kbuf.at[1], loc_s.at[1])
    lv = pltpu.make_async_copy(v_hbm, vbuf.at[1], loc_s.at[2])
    lp = pltpu.make_async_copy(kp_hbm, kpraw.at[1], loc_s.at[3])
    for cp in (lq, lk, lv, lp):
        cp.start()

    barrier = pltpu.get_barrier_semaphore()
    peers = 0
    for r in range(1, 8):
        pl.semaphore_signal(
            barrier, inc=1, device_id={"ctx": ctx_at(r // 4, r % 4), "tp": t}, device_id_type=MESH
        )
        pl.semaphore_signal(
            barrier, inc=1, device_id={"ctx": c, "tp": (t + r) % 8}, device_id_type=MESH
        )
        pl.semaphore_signal(
            barrier, inc=1, device_id={"ctx": across, "tp": (t + r) % 8}, device_id_type=MESH
        )
        peers += 3
    pl.semaphore_signal(barrier, inc=1, device_id={"ctx": partner, "tp": t}, device_id_type=MESH)
    pl.semaphore_wait(barrier, peers + 1)

    kv = [
        remote(k_hbm, kbuf.at[0], kv_ss.at[0], kv_rs.at[0], ctx=partner, tp=t),
        remote(v_hbm, vbuf.at[0], kv_ss.at[1], kv_rs.at[1], ctx=partner, tp=t),
        remote(kp_hbm, kpraw.at[0], kv_ss.at[2], kv_rs.at[2], ctx=partner, tp=t),
    ]

    def q_copy(r):
        return remote(
            q_hbm, q_all.at[r], q_ss.at[r], q_rs.at[r], ctx=ctx_at(r // 4, 4 - hop(r)), tp=t
        )

    kv[2].start()
    for r in (1, 2, 3, 4):
        q_copy(r).start()
    kv[0].start()
    kv[1].start()

    def q_forward(r):
        return remote(q_all.at[r], q_all.at[r + 4], q_ss.at[r + 4], q_rs.at[r + 4], ctx=across, tp=t)

    own_rows = pl.multiple_of(core * 1024 + z * 256, 256)

    def own_weight(j, which):
        src = (gate_hbm, up_hbm)[which]
        return pltpu.make_async_copy(
            src.at[:, pl.ds(j * CW, CW)],
            wbuf.at[j, pl.ds(own_rows, 256), pl.ds(which * CW, CW)],
            wl_s.at[2 * j + which],
        )

    for j in range(CHUNKS):
        own_weight(j, 0).start()
        own_weight(j, 1).start()
    def feature(half):
        return pl.ds(pl.multiple_of(half * 2048 + t * 256, 256), 256)

    lres = pltpu.make_async_copy(resid_hbm.at[:, feature(xh)], resid.at[0], loc_s.at[4])
    lgain = pltpu.make_async_copy(gain_hbm.at[feature(xh)], gain_buf, loc_s.at[5])
    rres = remote(
        resid_hbm.at[:, feature(1 - xh)], resid.at[1], kv_ss.at[3], kv_rs.at[3], ctx=across, tp=t
    )
    rres.start()
    lres.start()
    lgain.start()

    def ow_copy(s):
        return pltpu.make_async_copy(ow_hbm.at[:, pl.ds(s * 256, 256)], ow.at[s], ow_s.at[s])

    for s in range(16):
        ow_copy(s).start()

    def block(zz):
        return pl.multiple_of(core * 1024 + ((zz + 4) % 4) * 256, 256)

    def direct(j, way):
        rows = pl.ds(own_rows, 256)
        return remote(
            wbuf.at[j, rows],
            wbuf.at[j, rows],
            d_ss.at[way, j],
            d_rs.at[way, j],
            ctx=(up_z, down_z)[way],
            tp=t,
        )

    def direct_both(j):
        direct(j, 0).start()
        direct(j, 1).start()

    def direct_arrival(j, way):
        rows = pl.ds(block(z - 1 if way == 0 else z + 1), 256)
        return remote(
            wbuf.at[j, rows], wbuf.at[j, rows], d_ss.at[way, j], d_rs.at[way, j], ctx=up_z, tp=t
        )

    def forward(j, way):
        at = wbuf.at[j, pl.ds(block(z - 1 if way == 0 else z + 1), 256), pl.ds(way * CW, CW)]
        return remote(at, at, f_ss.at[way, j], f_rs.at[way, j], ctx=(up_z, down_z)[way], tp=t)

    def forward_arrival(j, way):
        at = wbuf.at[j, pl.ds(block(z + 2), 256), pl.ds(way * CW, CW)]
        return remote(at, at, f_ss.at[way, j], f_rs.at[way, j], ctx=up_z, tp=t)

    def pass_on(j):
        for way in (0, 1):
            direct_arrival(j, way).wait_recv()
        for way in (0, 1):
            forward(j, way).start()

    def relay(j):
        at = wbuf.at[j, pl.ds(pl.multiple_of(core * 1024, 1024), 1024)]
        return remote(at, at, r_ss.at[j], r_rs.at[j], ctx=partner, tp=t)

    def relay_arrival(j):
        at = wbuf.at[j, pl.ds(pl.multiple_of((1 - core) * 1024, 1024), 1024)]
        return remote(at, at, r_ss.at[j], r_rs.at[j], ctx=partner, tp=t)

    def hand_over(j):
        for way in (0, 1):
            forward_arrival(j, way).wait_recv()
        relay(j).start()

    def prepare(half):
        def turn(a, _):
            rows = pl.ds(pl.multiple_of(a * 128, 128), 128)
            vt[half, :, rows] = jnp.transpose(vbuf[half, rows, :].astype(F32)).astype(BF16)
            places = jnp.broadcast_to(kpraw[half, pl.ds(a, 1), :].astype(F32), (128, 128))
            kposb[half, rows, :] = jnp.transpose(places)
            return 0

        lax.fori_loop(0, 16, turn, 0, unroll=4)

    cvec[...] = jnp.exp2(jnp.broadcast_to(exps_ref[0:1, 0:1], (8, 128)).astype(F32)) * BASE
    acc_u[...] = jnp.zeros_like(acc_u)
    acc_s[...] = jnp.zeros_like(acc_s)
    for cp in (lq, lk, lv, lp):
        cp.wait()
    prepare(1)

    def qk(i, j, buf, mref):
        r = turn_owner((i + 1) // 2)
        half = (i + 1) % 2
        owner = ctx_at(r // 4, hop(r))
        qpos = qp_ref[pl.ds(owner, 1), :].astype(F32)
        qc = jnp.concatenate([q_all[r, :, h * HD : (h + 1) * HD] for h in range(4)], axis=0)
        s = lax.dot_general(
            kbuf[half, j * KT : (j + 1) * KT], qc, NT, preferred_element_type=F32
        )
        visible = kposb[half, j * KT : (j + 1) * KT] <= qpos
        s = jnp.concatenate(
            [jnp.where(visible, s[:, h * HD : (h + 1) * HD], LOW) for h in range(4)], axis=1
        )
        buf[...] = s
        mref[...] = jnp.max(s, axis=0, keepdims=True)

    def pv(i, j, buf, mref, state):
        half = (i + 1) % 2
        factor = cvec[0:1, 0:1]
        top = jnp.maximum(state[0], mref[...])
        p = jnp.exp2((buf[...] - top) * factor)
        total = jnp.sum(p, axis=0, keepdims=True)
        out = lax.dot_general(
            vt[half, :, j * KT : (j + 1) * KT], p.astype(BF16), NN, preferred_element_type=F32
        )
        keep = jnp.exp2((state[0] - top) * factor)
        return (top, state[1] * keep + total, state[2] * keep + out)

    def u_copy(r):
        return remote(usend.at[r], urecv.at[r], u_ss.at[r], u_rs.at[r], ctx=ctx_at(0, hop(r)), tp=t)

    def s_copy(r):
        return remote(ssend.at[r], srecv.at[r], st_ss.at[r], st_rs.at[r], ctx=ctx_at(0, hop(r)), tp=t)

    def u_across(r):
        return remote(usend.at[r], uhalf.at[r - 4], u_ss.at[r], uh_rs.at[r - 4], ctx=across, tp=t)

    def s_across(r):
        return remote(ssend.at[r], shalf.at[r - 4], st_ss.at[r], sh_rs.at[r - 4], ctx=across, tp=t)

    def combine(r):
        s_across(r + 4).wait_recv()
        u_across(r + 4).wait_recv()
        factor = cvec[0:1, 0:1]
        mine, theirs = ssend[r, 0:1, :], shalf[r, 0:1, :]
        top = jnp.maximum(mine, theirs)
        keep, add = jnp.exp2((mine - top) * factor), jnp.exp2((theirs - top) * factor)
        ssend[r, 0:1, :] = top
        ssend[r, 1:2, :] = ssend[r, 1:2, :] * keep + shalf[r, 1:2, :] * add
        usend[r] = (usend[r].astype(F32) * keep + uhalf[r].astype(F32) * add).astype(BF16)
        s_copy(r).start()
        u_copy(r).start()

    qk(0, 0, sa, ma)

    def step(i, _):
        odd = i % 2
        r = turn_owner((i + 1) // 2)
        r_next = turn_owner((i + 2) // 2)

        @pl.when(i == 0)
        def _():
            for cp in kv:
                cp.wait_recv()
            prepare(0)

        for n in range(3):

            @pl.when(i == 11 + 2 * n)
            def _(n=n):
                combine(n + 1)

        @pl.when((odd == 0) & (i < 14))
        def _():
            q_copy(r_next).wait_recv()

        @pl.when((odd == 0) & (i < 6))
        def _():
            q_forward(r_next).start()

        for n in range(EARLY):

            @pl.when(i == 3 * n)
            def _(n=n):
                own_weight(n, 0).wait()
                own_weight(n, 1).wait()
                direct_both(n)

        before = jnp.where(odd == 1, LOW, acc_s[0:1, :])
        before = jnp.where(i == 0, LOW, before)
        state = (before, acc_s[1:2, :], acc_u[...])
        qk(i, 1, sb, mb)
        state = pv(i, 0, sa, ma, state)
        qk(i + 1, 0, sa, ma)
        state = pv(i, 1, sb, mb, state)
        acc_s[0:1, :] = state[0]
        acc_s[1:2, :] = state[1]
        acc_u[...] = state[2]

        @pl.when(odd == 0)
        def _():
            usend[r] = acc_u[...].astype(BF16)
            ssend[r] = acc_s[...]

        @pl.when((odd == 0) & (i > 6))
        def _():
            s_across(r).start()
            u_across(r).start()

        return 0

    lax.fori_loop(0, 16, step, 0)

    for j in range(EARLY, CHUNKS):
        for which in (0, 1):
            own_weight(j, which).wait()
    for j in range(EARLY, CHUNKS):
        direct_both(j)
        if j < CHUNKS - 1:
            pass_on(j - EARLY)

    for r in (1, 2, 3):
        s_copy(r).wait_recv()
    s_across(4).wait_recv()
    tops = [acc_s[0:1, :], ssend[0, 0:1, :], shalf[0, 0:1, :]] + [srecv[r, 0:1, :] for r in (1, 2, 3)]
    sums = [acc_s[1:2, :], ssend[0, 1:2, :], shalf[0, 1:2, :]] + [srecv[r, 1:2, :] for r in (1, 2, 3)]
    top = functools.reduce(jnp.maximum, tops)
    factor = cvec[0:1, 0:1]
    shares = [jnp.exp2((m - top) * factor) for m in tops]
    total = functools.reduce(jnp.add, [w * l for w, l in zip(shares, sums)])
    merged = acc_u[...] * shares[0] + usend[0].astype(F32) * shares[1]
    u_across(4).wait_recv()
    merged = merged + uhalf[0].astype(F32) * shares[2]
    for r in (1, 2, 3):
        u_copy(r).wait_recv()
        merged = merged + urecv[r].astype(F32) * shares[r + 2]
    value_factor = jnp.exp2(jnp.broadcast_to(exps_ref[0:1, 1:2], (8, 128)).astype(F32))[0:1, 0:1]
    merged = merged * (value_factor / total)
    attention = jnp.concatenate(
        [jnp.transpose(merged[:, h * HD : (h + 1) * HD]) for h in range(4)], axis=1
    ).astype(BF16)

    for n in range(16):
        ow_copy(n).wait()

    def p_copy(side, k):
        return remote(
            rs_send.at[side, k],
            rs_recv.at[side, k],
            p_ss.at[side, k],
            p_rs.at[side, k],
            ctx=(c, across)[side],
            tp=(t + k) % 8,
        )

    def product(side, k):
        half = (xh, 1 - xh)[side]
        return lax.dot_general(attention, ow[half * 8 + (t + k) % 8], NN, preferred_element_type=F32)

    for k in (0, 4, 3, 5, 2, 6, 1, 7):
        rs_send[1, k] = product(1, k).astype(BF16)
        p_copy(1, k).start()
    for k in (4, 3, 5, 2, 6, 1, 7):
        rs_send[0, k] = product(0, k).astype(BF16)
        p_copy(0, k).start()
    own = product(0, 0)
    lres.wait()
    lgain.wait()
    rres.wait_recv()
    gain = jnp.broadcast_to(gain_buf[...].astype(F32).reshape(1, 256), (128, 256))

    def g_copy(side, k):
        lane = pl.ds(pl.multiple_of((t // 2) * 256, 256), 256)
        return remote(
            gsend.at[side],
            gbuf.at[t % 2, side, :, lane],
            g_ss.at[side, k],
            g_rs.at[side, k],
            ctx=c,
            tp=(t + k) % 8,
        )

    def spread(side):
        stream = resid[side].astype(F32)
        if side == 0:
            stream = stream + own
        for k in range(1 - side, 8):
            p_copy(side, k).wait_recv()
            stream = stream + rs_recv[side, k].astype(F32)
        scaled = (stream * gain).astype(BF16)
        gsend[side] = scaled
        for k in (4, 3, 5, 2, 6, 1, 7):
            g_copy(side, k).start()
        lane = pl.ds(pl.multiple_of((t // 2) * 256, 256), 256)
        gbuf[t % 2, side, :, lane] = scaled
        sq_send[side] = lax.dot_general(
            jnp.ones((8, 256), F32),
            stream * stream,
            NT,
            preferred_element_type=F32,
            precision=lax.Precision.HIGHEST,
        )

    def sq_copy(k):
        return remote(sq_send, sq_recv.at[k], sq_ss.at[k], sq_rs.at[k], ctx=c, tp=(t + k) % 8)

    def sq_swap():
        return remote(sq_recv.at[0, 1], sq_other, sq_ss.at[0], sq_rs.at[0], ctx=across, tp=t)

    spread(1)
    pass_on(3)
    spread(0)
    for k in range(1, 8):
        sq_copy(k).start()
    pass_on(4)
    hand_over(0)

    for side in (1, 0):
        squares = sq_send[side]
        for k in range(1, 8):
            if side == 1:
                sq_copy(k).wait_recv()
            squares = squares + sq_recv[k, side]
        sq_recv[0, side] = squares
        if side == 1:
            sq_swap().start()

    def g_arrival(side, k):
        at = gbuf.at[0, side, :, pl.ds(0, 256)]
        return remote(at, at, g_ss.at[side, k], g_rs.at[side, k], ctx=across, tp=t)

    def x_copy(j):
        return remote(xsend.at[j], xrecv.at[j], x_ss.at[j], x_rs.at[j], ctx=across, tp=t)

    def finish(j):
        x_copy(j).wait_recv()
        both = (pown[j] + xrecv[j].astype(F32)) * scale[:, 0:1]
        gate = both[:, :CW]
        up = both[:, CW:]
        out_ref[:, pl.ds(pl.multiple_of(j * CW, CW), CW)] = (gate / (1.0 + jnp.exp(-gate)) * up).astype(BF16)

    def half_product(j, side):
        return lax.dot_general(
            gbuf[0, side], wbuf[j, 0:1024, :], NN, preferred_element_type=F32
        ) + lax.dot_general(
            gbuf[1, side], wbuf[j, 1024:2048, :], NN, preferred_element_type=F32
        )

    for k in range(1, 8):
        g_arrival(1, k).wait_recv()

    def chunk(j, _):
        @pl.when(j < 2)
        def _():
            pass_on(j + 5)

        @pl.when(j < CHUNKS - 1)
        def _():
            hand_over(j + 1)

        relay_arrival(j).wait_recv()
        xsend[j] = half_product(j, 1).astype(BF16)
        x_copy(j).start()

        @pl.when(j == 0)
        def _():
            for k in range(1, 8):
                g_arrival(0, k).wait_recv()
            sq_swap().wait_recv()
            squares = sq_recv[0, 0, 0:1, :] + sq_other[0:1, :]
            scale_row = lax.rsqrt(squares * (1.0 / 4096.0) + 1e-05)
            scale[...] = jnp.transpose(jnp.broadcast_to(scale_row, (128, 128)))

        pown[j] = half_product(j, 0)

        @pl.when(j >= 2)
        def _():
            finish(j - 2)

        return 0

    lax.fori_loop(0, CHUNKS, chunk, 0)
    finish(CHUNKS - 2)
    finish(CHUNKS - 1)

    for cp in kv:
        cp.wait_send()
    rres.wait_send()
    for r in (1, 2, 3, 4):
        q_copy(r).wait_send()
    for r in (1, 2, 3):
        q_forward(r).wait_send()
        u_copy(r).wait_send()
        s_copy(r).wait_send()
    for r in (4, 5, 6, 7):
        u_across(r).wait_send()
        s_across(r).wait_send()
    for k in range(8):
        p_copy(1, k).wait_send()
        if k:
            p_copy(0, k).wait_send()
            g_copy(1, k).wait_send()
            g_copy(0, k).wait_send()
            sq_copy(k).wait_send()
    sq_swap().wait_send()
    for j in range(CHUNKS):
        for way in (0, 1):
            direct(j, way).wait_send()
            forward(j, way).wait_send()
        relay(j).wait_send()
        x_copy(j).wait_send()


def body(
    queries,
    key_cache,
    value_cache,
    scale_exps,
    query_pos,
    key_pos,
    resid,
    out_weight,
    norm_gain,
    gate_weight,
    up_weight,
):
    vmem = pl.BlockSpec(memory_space=pltpu.VMEM)
    hbm = pl.BlockSpec(memory_space=pl.ANY)
    V = pltpu.VMEM
    dma = pltpu.SemaphoreType.DMA
    return pl.pallas_call(
        kernel,
        out_shape=jax.ShapeDtypeStruct((128, 1792), BF16),
        in_specs=[hbm, hbm, hbm, vmem, vmem, hbm, hbm, hbm, hbm, hbm, hbm],
        out_specs=vmem,
        scratch_shapes=[
            V((8, 128, 512), BF16),
            V((2, 2048, 128), BF16),
            V((2, 2048, 128), BF16),
            V((2, 128, 2048), BF16),
            V((2, 16, 128), jnp.int32),
            V((2, 2048, 128), F32),
            V((KT, 512), F32),
            V((KT, 512), F32),
            V((1, 512), F32),
            V((1, 512), F32),
            V((128, 512), F32),
            V((8, 512), F32),
            V((8, 128), F32),
            V((8, 128, 512), BF16),
            V((8, 8, 512), F32),
            V((4, 128, 512), BF16),
            V((4, 8, 512), F32),
            V((4, 128, 512), BF16),
            V((4, 8, 512), F32),
            V((16, 512, 256), BF16),
            V((2, 128, 256), BF16),
            V((256,), BF16),
            V((2, 8, 128, 256), BF16),
            V((2, 8, 128, 256), BF16),
            V((2, 8, 128), F32),
            V((8, 2, 8, 128), F32),
            V((8, 128), F32),
            V((2, 128, 256), BF16),
            V((2, 2, 128, 1024), BF16),
            V((CHUNKS, 2048, 2 * CW), BF16),
            V((CHUNKS, 128, 2 * CW), BF16),
            V((CHUNKS, 128, 2 * CW), BF16),
            V((CHUNKS, 128, 2 * CW), F32),
            V((128, 128), F32),
            dma((8,)),
            dma((8,)),
            dma((4,)),
            dma((4,)),
            dma((6,)),
            dma((16,)),
            dma((2 * CHUNKS,)),
            dma((8,)),
            dma((4,)),
            dma((8,)),
            dma((4,)),
            dma((4,)),
            dma((4,)),
            dma((2, CHUNKS)),
            dma((2, CHUNKS)),
            dma((2, CHUNKS)),
            dma((2, CHUNKS)),
            dma((CHUNKS,)),
            dma((CHUNKS,)),
            dma((2, 8)),
            dma((2, 8)),
            dma((8,)),
            dma((8,)),
            dma((2, 8)),
            dma((2, 8)),
            dma((CHUNKS,)),
            dma((CHUNKS,)),
        ],
        compiler_params=pltpu.CompilerParams(
            collective_id=0, has_side_effects=True, vmem_limit_bytes=60 * 2**20
        ),
        cost_estimate=pl.CostEstimate(
            flops=18_000_000_000, bytes_accessed=16_000_000, transcendentals=17_000_000
        ),
    )(
        queries,
        key_cache,
        value_cache,
        scale_exps.T,
        query_pos.reshape(16, 128),
        key_pos.reshape(16, 128),
        resid,
        out_weight,
        norm_gain,
        gate_weight,
        up_weight,
    )


def solution(mesh):
    placed = (
        P("ctx", "tp"),
        P("ctx", "tp"),
        P("ctx", "tp"),
        P(None, "tp"),
        P(),
        P("ctx"),
        P("ctx", None),
        P("tp", None),
        P(),
        P("ctx", "tp"),
        P("ctx", "tp"),
    )
    return jax.shard_map(
        body, mesh=mesh, in_specs=placed, out_specs=P("ctx", "tp"), check_vma=False
    )
```

```python
import functools
import math

import jax
import jax.numpy as jnp
from jax import lax
from jax.experimental import pallas as pl
from jax.experimental.pallas import tpu as pltpu
from jax.sharding import PartitionSpec as P

HD = 128
NT = (((1,), (1,)), ((), ()))
NN = (((1,), (0,)), ((), ()))
MESH = pl.DeviceIdType.MESH
LOW = -1e30
BASE = math.log2(math.e) / math.sqrt(HD)
F32 = jnp.float32
BF16 = jnp.bfloat16
KT = 1024
CHUNKS = 7
CW = 256
EARLY = 4


def hop(r):
    low = r % 4
    return ((low * (low + 1)) // 2) % 4


def turn_owner(n):
    n = n % 8
    late, m = n // 4, n % 4
    return late * (7 - 2 * (m % 2) - m // 2) + (1 - late) * n


def kernel(
    q_hbm,
    k_hbm,
    v_hbm,
    exps_ref,
    qp_ref,
    kp_hbm,
    resid_hbm,
    ow_hbm,
    gain_hbm,
    gate_hbm,
    up_hbm,
    out_ref,
    q_all,
    kbuf,
    vbuf,
    vt,
    kpraw,
    kposb,
    sa,
    sb,
    ma,
    mb,
    acc_u,
    acc_s,
    cvec,
    usend,
    ssend,
    urecv,
    srecv,
    uhalf,
    shalf,
    ow,
    resid,
    gain_buf,
    rs_send,
    rs_recv,
    sq_send,
    sq_recv,
    sq_other,
    gsend,
    gbuf,
    wbuf,
    xsend,
    xrecv,
    pown,
    scale,
    q_ss,
    q_rs,
    kv_ss,
    kv_rs,
    loc_s,
    ow_s,
    wl_s,
    u_ss,
    u_rs,
    st_ss,
    st_rs,
    uh_rs,
    sh_rs,
    d_ss,
    d_rs,
    f_ss,
    f_rs,
    r_ss,
    r_rs,
    p_ss,
    p_rs,
    sq_ss,
    sq_rs,
    g_ss,
    g_rs,
    x_ss,
    x_rs,
):
    c = lax.axis_index("ctx")
    t = lax.axis_index("tp")
    core = c % 2
    z = (c // 2) % 4
    xh = c // 8

    def ctx_at(dx, dz, dc=0):
        return ((xh + dx) % 2) * 8 + ((z + dz + 4) % 4) * 2 + (core + dc) % 2

    partner = ctx_at(0, 0, 1)
    across = ctx_at(1, 0)
    up_z = ctx_at(0, 1)
    down_z = ctx_at(0, 3)

    def remote(src, dst, ss, rs, **dev):
        return pltpu.make_async_remote_copy(
            src_ref=src, dst_ref=dst, send_sem=ss, recv_sem=rs, device_id=dev, device_id_type=MESH
        )

    lq = pltpu.make_async_copy(q_hbm, q_all.at[0], loc_s.at[0])
    lk = pltpu.make_async_copy(k_hbm, kbuf.at[1], loc_s.at[1])
    lv = pltpu.make_async_copy(v_hbm, vbuf.at[1], loc_s.at[2])
    lp = pltpu.make_async_copy(kp_hbm, kpraw.at[1], loc_s.at[3])
    for cp in (lq, lk, lv, lp):
        cp.start()

    barrier = pltpu.get_barrier_semaphore()
    peers = 0
    for r in range(1, 8):
        pl.semaphore_signal(
            barrier, inc=1, device_id={"ctx": ctx_at(r // 4, r % 4), "tp": t}, device_id_type=MESH
        )
        pl.semaphore_signal(
            barrier, inc=1, device_id={"ctx": c, "tp": (t + r) % 8}, device_id_type=MESH
        )
        pl.semaphore_signal(
            barrier, inc=1, device_id={"ctx": across, "tp": (t + r) % 8}, device_id_type=MESH
        )
        peers += 3
    pl.semaphore_signal(barrier, inc=1, device_id={"ctx": partner, "tp": t}, device_id_type=MESH)
    pl.semaphore_wait(barrier, peers + 1)

    kv = [
        remote(k_hbm, kbuf.at[0], kv_ss.at[0], kv_rs.at[0], ctx=partner, tp=t),
        remote(v_hbm, vbuf.at[0], kv_ss.at[1], kv_rs.at[1], ctx=partner, tp=t),
        remote(kp_hbm, kpraw.at[0], kv_ss.at[2], kv_rs.at[2], ctx=partner, tp=t),
    ]

    def q_copy(r):
        return remote(
            q_hbm, q_all.at[r], q_ss, q_rs.at[r], ctx=ctx_at(r // 4, 4 - hop(r)), tp=t
        )

    kv[2].start()
    for r in (1, 2, 3, 4):
        q_copy(r).start()
    kv[0].start()
    kv[1].start()

    def q_forward(r):
        return remote(q_all.at[r], q_all.at[r + 4], q_ss, q_rs.at[r + 4], ctx=across, tp=t)

    own_rows = pl.multiple_of(core * 1024 + z * 256, 256)

    def own_weight(j, which):
        src = (gate_hbm, up_hbm)[which]
        return pltpu.make_async_copy(
            src.at[:, pl.ds(j * CW, CW)],
            wbuf.at[j, pl.ds(own_rows, 256), pl.ds(which * CW, CW)],
            wl_s,
        )

    for j in range(CHUNKS):
        own_weight(j, 0).start()
        own_weight(j, 1).start()
    def feature(half):
        return pl.ds(pl.multiple_of(half * 2048 + t * 256, 256), 256)

    lres = pltpu.make_async_copy(resid_hbm.at[:, feature(xh)], resid.at[0], loc_s.at[4])
    lgain = pltpu.make_async_copy(gain_hbm.at[feature(xh)], gain_buf, loc_s.at[5])
    rres = remote(
        resid_hbm.at[:, feature(1 - xh)], resid.at[1], kv_ss.at[3], kv_rs.at[3], ctx=across, tp=t
    )
    rres.start()
    lres.start()
    lgain.start()

    def ow_copy(s):
        return pltpu.make_async_copy(ow_hbm.at[:, pl.ds(s * 256, 256)], ow.at[s], ow_s)

    for s in range(16):
        ow_copy(s).start()

    def block(zz):
        return pl.multiple_of(core * 1024 + ((zz + 4) % 4) * 256, 256)

    def direct(j, way):
        rows = pl.ds(own_rows, 256)
        return remote(
            wbuf.at[j, rows],
            wbuf.at[j, rows],
            d_ss,
            d_rs.at[j],
            ctx=(up_z, down_z)[way],
            tp=t,
        )

    def direct_both(j):
        direct(j, 0).start()
        direct(j, 1).start()

    def arrived(ref, sem):
        remote(ref, ref, d_ss, sem, ctx=partner, tp=t).wait_recv()

    def left(ref, sem):
        remote(ref, ref, sem, d_rs.at[0], ctx=partner, tp=t).wait_send()

    def forward(j, way):
        at = wbuf.at[j, pl.ds(block(z - 1 if way == 0 else z + 1), 256), pl.ds(way * CW, CW)]
        return remote(at, at, f_ss, f_rs.at[j], ctx=(up_z, down_z)[way], tp=t)

    def relay(j, dz):
        at = wbuf.at[j, pl.ds(block(z + dz), 256)]
        return remote(at, at, r_ss, r_rs.at[j], ctx=partner, tp=t)

    def pass_on(j):
        arrived(wbuf.at[j, 0:512], d_rs.at[j])
        for way in (0, 1):
            forward(j, way).start()
        for dz in (0, 1, 3):
            relay(j, dz).start()

    def hand_over(j):
        arrived(wbuf.at[j, 0:256], f_rs.at[j])
        relay(j, 2).start()

    def prepare(half):
        def turn(a, _):
            rows = pl.ds(pl.multiple_of(a * 128, 128), 128)
            vt[half, :, rows] = jnp.transpose(vbuf[half, rows, :].astype(F32)).astype(BF16)
            places = jnp.broadcast_to(kpraw[half, pl.ds(a, 1), :].astype(F32), (128, 128))
            kposb[half, rows, :] = jnp.transpose(places)
            return 0

        lax.fori_loop(0, 16, turn, 0, unroll=4)

    cvec[...] = jnp.exp2(jnp.broadcast_to(exps_ref[0:1, 0:1], (8, 128)).astype(F32)) * BASE
    acc_u[...] = jnp.zeros_like(acc_u)
    acc_s[...] = jnp.zeros_like(acc_s)
    for cp in (lq, lk, lv, lp):
        cp.wait()
    prepare(1)

    def qk(i, j, buf, mref):
        r = turn_owner((i + 1) // 2)
        half = (i + 1) % 2
        owner = ctx_at(r // 4, hop(r))
        qpos = qp_ref[pl.ds(owner, 1), :].astype(F32)
        qc = jnp.concatenate([q_all[r, :, h * HD : (h + 1) * HD] for h in range(4)], axis=0)
        s = lax.dot_general(
            kbuf[half, j * KT : (j + 1) * KT], qc, NT, preferred_element_type=F32
        )
        visible = kposb[half, j * KT : (j + 1) * KT] <= qpos
        s = jnp.concatenate(
            [jnp.where(visible, s[:, h * HD : (h + 1) * HD], LOW) for h in range(4)], axis=1
        )
        buf[...] = s
        mref[...] = jnp.max(s, axis=0, keepdims=True)

    def pv(i, j, buf, mref, state):
        half = (i + 1) % 2
        factor = cvec[0:1, 0:1]
        top = jnp.maximum(state[0], mref[...])
        p = jnp.exp2((buf[...] - top) * factor)
        total = jnp.sum(p, axis=0, keepdims=True)
        out = lax.dot_general(
            vt[half, :, j * KT : (j + 1) * KT], p.astype(BF16), NN, preferred_element_type=F32
        )
        keep = jnp.exp2((state[0] - top) * factor)
        return (top, state[1] * keep + total, state[2] * keep + out)

    def u_copy(r):
        return remote(usend.at[r], urecv.at[r], u_ss, u_rs, ctx=ctx_at(0, hop(r)), tp=t)

    def s_copy(r):
        return remote(ssend.at[r], srecv.at[r], st_ss, st_rs, ctx=ctx_at(0, hop(r)), tp=t)

    def u_across(r):
        return remote(usend.at[r], uhalf.at[r - 4], u_ss, uh_rs.at[r - 4], ctx=across, tp=t)

    def s_across(r):
        return remote(ssend.at[r], shalf.at[r - 4], st_ss, sh_rs.at[r - 4], ctx=across, tp=t)

    def combine(r):
        s_across(r + 4).wait_recv()
        u_across(r + 4).wait_recv()
        factor = cvec[0:1, 0:1]
        mine, theirs = ssend[r, 0:1, :], shalf[r, 0:1, :]
        top = jnp.maximum(mine, theirs)
        keep, add = jnp.exp2((mine - top) * factor), jnp.exp2((theirs - top) * factor)
        ssend[r, 0:1, :] = top
        ssend[r, 1:2, :] = ssend[r, 1:2, :] * keep + shalf[r, 1:2, :] * add
        usend[r] = (usend[r].astype(F32) * keep + uhalf[r].astype(F32) * add).astype(BF16)
        s_copy(r).start()
        u_copy(r).start()

    qk(0, 0, sa, ma)

    def step(i, _):
        odd = i % 2
        r = turn_owner((i + 1) // 2)
        r_next = turn_owner((i + 2) // 2)

        for n, (at, r_z) in enumerate(((12, 3), (14, 1), (15, 2))):

            @pl.when(i == at)
            def _(r_z=r_z):
                combine(r_z)

        for n in range(EARLY):

            @pl.when(i == 3 * n)
            def _(n=n):
                if n == 0:
                    mine = wbuf.at[:, pl.ds(own_rows, 256)]
                    pltpu.make_async_copy(mine, mine, wl_s).wait()
                direct_both(n)

        @pl.when(i == 0)
        def _():
            for cp in kv:
                cp.wait_recv()
            prepare(0)

        @pl.when((odd == 0) & (i < 14))
        def _():
            q_copy(r_next).wait_recv()

        @pl.when((odd == 0) & (i < 6))
        def _():
            q_forward(r_next).start()

        before = jnp.where(odd == 1, LOW, acc_s[0:1, :])
        before = jnp.where(i == 0, LOW, before)
        state = (before, acc_s[1:2, :], acc_u[...])
        qk(i, 1, sb, mb)
        state = pv(i, 0, sa, ma, state)
        qk(i + 1, 0, sa, ma)
        state = pv(i, 1, sb, mb, state)
        acc_s[0:1, :] = state[0]
        acc_s[1:2, :] = state[1]
        acc_u[...] = state[2]

        @pl.when(odd == 0)
        def _():
            usend[r] = acc_u[...].astype(BF16)
            ssend[r] = acc_s[...]

        @pl.when((odd == 0) & (i > 6))
        def _():
            s_across(r).start()
            u_across(r).start()

        return 0

    lax.fori_loop(0, 16, step, 0)

    for j in range(EARLY, CHUNKS):
        direct_both(j)
        pass_on(j - EARLY)

    arrived(srecv.at[1:4], st_rs)
    s_across(4).wait_recv()
    tops = [acc_s[0:1, :], ssend[0, 0:1, :], shalf[0, 0:1, :]] + [srecv[r, 0:1, :] for r in (1, 2, 3)]
    sums = [acc_s[1:2, :], ssend[0, 1:2, :], shalf[0, 1:2, :]] + [srecv[r, 1:2, :] for r in (1, 2, 3)]
    top = functools.reduce(jnp.maximum, tops)
    factor = cvec[0:1, 0:1]
    shares = [jnp.exp2((m - top) * factor) for m in tops]
    total = functools.reduce(jnp.add, [w * l for w, l in zip(shares, sums)])
    merged = acc_u[...] * shares[0] + usend[0].astype(F32) * shares[1]
    u_across(4).wait_recv()
    merged = merged + uhalf[0].astype(F32) * shares[2]
    arrived(urecv.at[1:4], u_rs)
    for r in (1, 2, 3):
        merged = merged + urecv[r].astype(F32) * shares[r + 2]
    value_factor = jnp.exp2(jnp.broadcast_to(exps_ref[0:1, 1:2], (8, 128)).astype(F32))[0:1, 0:1]
    merged = merged * (value_factor / total)
    attention = jnp.concatenate(
        [jnp.transpose(merged[:, h * HD : (h + 1) * HD]) for h in range(4)], axis=1
    ).astype(BF16)

    pltpu.make_async_copy(ow, ow, ow_s).wait()

    def p_copy(side, k):
        return remote(
            rs_send.at[side, k],
            rs_recv.at[side, k],
            p_ss.at[side],
            p_rs.at[side],
            ctx=(c, across)[side],
            tp=(t + k) % 8,
        )

    def product(side, k):
        half = (xh, 1 - xh)[side]
        return lax.dot_general(attention, ow[half * 8 + (t + k) % 8], NN, preferred_element_type=F32)

    for k in (0, 4, 3, 5, 2, 6, 1, 7):
        rs_send[1, k] = product(1, k).astype(BF16)
        p_copy(1, k).start()
    for k in (4, 3, 5, 2, 6, 1, 7):
        rs_send[0, k] = product(0, k).astype(BF16)
        p_copy(0, k).start()
    own = product(0, 0)
    lres.wait()
    lgain.wait()
    rres.wait_recv()
    gain = jnp.broadcast_to(gain_buf[...].astype(F32).reshape(1, 256), (128, 256))

    def g_copy(side, k):
        lane = pl.ds(pl.multiple_of((t // 2) * 256, 256), 256)
        return remote(
            gsend.at[side],
            gbuf.at[t % 2, side, :, lane],
            g_ss.at[side],
            g_rs.at[side],
            ctx=c,
            tp=(t + k) % 8,
        )

    def spread(side):
        stream = resid[side].astype(F32)
        if side == 0:
            stream = stream + own
        arrived(rs_recv.at[side, 1 - side : 8], p_rs.at[side])
        for k in range(1 - side, 8):
            stream = stream + rs_recv[side, k].astype(F32)
        scaled = (stream * gain).astype(BF16)
        gsend[side] = scaled
        for k in (4, 3, 5, 2, 6, 1, 7):
            g_copy(side, k).start()
        lane = pl.ds(pl.multiple_of((t // 2) * 256, 256), 256)
        gbuf[t % 2, side, :, lane] = scaled
        sq_send[side] = lax.dot_general(
            jnp.ones((8, 256), F32),
            stream * stream,
            NT,
            preferred_element_type=F32,
            precision=lax.Precision.HIGHEST,
        )

    def sq_copy(k):
        return remote(sq_send, sq_recv.at[k], sq_ss.at[0], sq_rs.at[0], ctx=c, tp=(t + k) % 8)

    def sq_swap():
        return remote(sq_recv.at[0, 1], sq_other, sq_ss.at[1], sq_rs.at[1], ctx=across, tp=t)

    spread(1)
    pass_on(3)
    spread(0)
    for k in range(1, 8):
        sq_copy(k).start()
    pass_on(4)
    hand_over(0)

    def swap_squares():
        arrived(sq_recv.at[1:8], sq_rs.at[0])
        for side in (1, 0):
            squares = sq_send[side]
            for k in range(1, 8):
                squares = squares + sq_recv[k, side]
            sq_recv[0, side] = squares
        sq_swap().start()

    def g_arrival(side):
        arrived(rs_recv.at[0, 1:8], g_rs.at[side])

    def x_copy(j):
        return remote(xsend.at[j], xrecv.at[j], x_ss, x_rs.at[j], ctx=across, tp=t)

    def finish(j):
        x_copy(j).wait_recv()
        both = (pown[j] + xrecv[j].astype(F32)) * scale[:, 0:1]
        gate = both[:, :CW]
        up = both[:, CW:]
        out_ref[:, pl.ds(pl.multiple_of(j * CW, CW), CW)] = (gate / (1.0 + jnp.exp(-gate)) * up).astype(BF16)

    def half_product(j, side):
        return lax.dot_general(
            gbuf[0, side], wbuf[j, 0:1024, :], NN, preferred_element_type=F32
        ) + lax.dot_general(
            gbuf[1, side], wbuf[j, 1024:2048, :], NN, preferred_element_type=F32
        )

    def drain():
        for cp in kv:
            cp.wait_send()
        rres.wait_send()
        left(q_all.at[1:8], q_ss)
        left(usend.at[1:8], u_ss)
        left(ssend.at[1:8], st_ss)
        left(rs_send.at[1], p_ss.at[1])
        for ref in (p_ss.at[0], g_ss.at[0], g_ss.at[1]):
            left(rs_send.at[0, 1:8], ref)
        left(sq_recv.at[1:8], sq_ss.at[0])
        sq_swap().wait_send()
        left(wbuf.at[:, 0:512], d_ss)
        left(wbuf.at[:, 0:256], f_ss)
        left(wbuf.at[:, 0:1024], r_ss)

    g_arrival(1)

    def chunk(j, _):
        @pl.when(j < 2)
        def _():
            pass_on(j + 5)

        @pl.when(j < CHUNKS - 1)
        def _():
            hand_over(j + 1)

        arrived(wbuf.at[j, 0:1024], r_rs.at[j])
        xsend[j] = half_product(j, 1).astype(BF16)
        x_copy(j).start()

        @pl.when(j == 2)
        def _():
            g_arrival(0)
            swap_squares()

        @pl.when(j >= 2)
        def _():
            pown[j - 2] = half_product(j - 2, 0)

        @pl.when(j == 4)
        def _():
            sq_swap().wait_recv()
            squares = sq_recv[0, 0, 0:1, :] + sq_other[0:1, :]
            scale_row = lax.rsqrt(squares * (1.0 / 4096.0) + 1e-05)
            scale[...] = jnp.transpose(jnp.broadcast_to(scale_row, (128, 128)))

        @pl.when(j >= 4)
        def _():
            finish(j - 4)

        return 0

    lax.fori_loop(0, CHUNKS, chunk, 0)

    drain()
    for j in range(CHUNKS - 4, CHUNKS):
        if j >= CHUNKS - 2:
            pown[j] = half_product(j, 0)
        finish(j)
    left(xsend, x_ss)


def body(
    queries,
    key_cache,
    value_cache,
    scale_exps,
    query_pos,
    key_pos,
    resid,
    out_weight,
    norm_gain,
    gate_weight,
    up_weight,
):
    vmem = pl.BlockSpec(memory_space=pltpu.VMEM)
    hbm = pl.BlockSpec(memory_space=pl.ANY)
    V = pltpu.VMEM
    dma = pltpu.SemaphoreType.DMA
    return pl.pallas_call(
        kernel,
        out_shape=pltpu.VMEM((128, 1792), BF16),
        in_specs=[hbm, hbm, hbm, vmem, vmem, hbm, hbm, hbm, hbm, hbm, hbm],
        out_specs=vmem,
        scratch_shapes=[
            V((8, 128, 512), BF16),
            V((2, 2048, 128), BF16),
            V((2, 2048, 128), BF16),
            V((2, 128, 2048), BF16),
            V((2, 16, 128), jnp.int32),
            V((2, 2048, 128), F32),
            V((KT, 512), F32),
            V((KT, 512), F32),
            V((1, 512), F32),
            V((1, 512), F32),
            V((128, 512), F32),
            V((8, 512), F32),
            V((8, 128), F32),
            V((8, 128, 512), BF16),
            V((8, 8, 512), F32),
            V((4, 128, 512), BF16),
            V((4, 8, 512), F32),
            V((4, 128, 512), BF16),
            V((4, 8, 512), F32),
            V((16, 512, 256), BF16),
            V((2, 128, 256), BF16),
            V((256,), BF16),
            V((2, 8, 128, 256), BF16),
            V((2, 8, 128, 256), BF16),
            V((2, 8, 128), F32),
            V((8, 2, 8, 128), F32),
            V((8, 128), F32),
            V((2, 128, 256), BF16),
            V((2, 2, 128, 1024), BF16),
            V((CHUNKS, 2048, 2 * CW), BF16),
            V((CHUNKS, 128, 2 * CW), BF16),
            V((CHUNKS, 128, 2 * CW), BF16),
            V((CHUNKS, 128, 2 * CW), F32),
            V((128, 128), F32),
            dma,
            dma((8,)),
            dma((4,)),
            dma((4,)),
            dma((6,)),
            dma,
            dma,
            dma,
            dma,
            dma,
            dma,
            dma((4,)),
            dma((4,)),
            dma,
            dma((CHUNKS,)),
            dma,
            dma((CHUNKS,)),
            dma,
            dma((CHUNKS,)),
            dma((2,)),
            dma((2,)),
            dma((2,)),
            dma((2,)),
            dma((2,)),
            dma((2,)),
            dma,
            dma((CHUNKS,)),
        ],
        compiler_params=pltpu.CompilerParams(
            collective_id=0, has_side_effects=True, vmem_limit_bytes=60 * 2**20
        ),
        cost_estimate=pl.CostEstimate(
            flops=18_000_000_000, bytes_accessed=16_000_000, transcendentals=17_000_000
        ),
    )(
        queries,
        key_cache,
        value_cache,
        scale_exps.T,
        query_pos.reshape(16, 128),
        key_pos.reshape(16, 128),
        resid,
        out_weight,
        norm_gain,
        gate_weight,
        up_weight,
    )


def solution(mesh):
    placed = (
        P("ctx", "tp"),
        P("ctx", "tp"),
        P("ctx", "tp"),
        P(None, "tp"),
        P(),
        P("ctx"),
        P("ctx", None),
        P("tp", None),
        P(),
        P("ctx", "tp"),
        P("ctx", "tp"),
    )
    return jax.shard_map(
        body, mesh=mesh, in_specs=placed, out_specs=P("ctx", "tp"), check_vma=False
    )
```

```python
import functools
import math

import jax
import jax.numpy as jnp
from jax import lax
from jax.experimental import pallas as pl
from jax.experimental.pallas import tpu as pltpu
from jax.sharding import PartitionSpec as P

HD = 128
NT = (((1,), (1,)), ((), ()))
NN = (((1,), (0,)), ((), ()))
MESH = pl.DeviceIdType.MESH
LOW = -1e30
BASE = math.log2(math.e) / math.sqrt(HD)
F32 = jnp.float32
BF16 = jnp.bfloat16
KT = 1024
CHUNKS = 14
CW = 128
LAG = 7


def hop(r):
    low = r % 4
    return ((low * (low + 1)) // 2) % 4


def turn_owner(n):
    n = n % 8
    return n + 3 * ((n + 6) // 8) - 4 * ((n + 3) // 8) - 2 * ((n + 2) // 8) - 2 * (n // 7)


def kernel(
    q_hbm,
    k_hbm,
    v_hbm,
    exps_ref,
    qp_ref,
    kp_hbm,
    resid_hbm,
    ow_hbm,
    gain_hbm,
    gate_hbm,
    up_hbm,
    out_ref,
    q_all,
    kbuf,
    vbuf,
    vt,
    kpraw,
    kposb,
    sa,
    sb,
    ma,
    mb,
    acc_u,
    acc_s,
    cvec,
    usend,
    ssend,
    urecv,
    srecv,
    uhalf,
    shalf,
    ow,
    resid,
    resid_own,
    gain_buf,
    gain_wide,
    rs_send,
    rs_recv,
    ws_send,
    ws_recv,
    swap_send,
    swap_recv,
    own,
    far_squares,
    own_squares,
    sq_recv,
    oq_recv,
    sq_other,
    gsend,
    gsend_wide,
    gbuf,
    wbuf,
    xsend,
    xrecv,
    pown,
    scale,
    q_ss,
    q_rs,
    kv_ss,
    kv_rs,
    loc_s,
    ow_s,
    wl_s,
    u_ss,
    u_rs,
    st_ss,
    st_rs,
    uh_rs,
    sh_rs,
    d_ss,
    d_rs,
    f_ss,
    f_rs,
    r_ss,
    r_rs,
    p_ss,
    p_rs,
    w_ss,
    w_rs,
    sw_ss,
    sw_rs,
    sq_ss,
    sq_rs,
    g_ss,
    g_rs,
    x_ss,
    x_rs,
):
    c = lax.axis_index("ctx")
    t = lax.axis_index("tp")
    core = c % 2
    z = (c // 2) % 4
    xh = c // 8

    def ctx_at(dx, dz, dc=0):
        return ((xh + dx) % 2) * 8 + ((z + dz + 4) % 4) * 2 + (core + dc) % 2

    partner = ctx_at(0, 0, 1)
    across = ctx_at(1, 0)
    up_z = ctx_at(0, 1)
    down_z = ctx_at(0, 3)

    def remote(src, dst, ss, rs, **dev):
        return pltpu.make_async_remote_copy(
            src_ref=src, dst_ref=dst, send_sem=ss, recv_sem=rs, device_id=dev, device_id_type=MESH
        )

    lq = pltpu.make_async_copy(q_hbm, q_all.at[0], loc_s.at[0])
    lk = pltpu.make_async_copy(k_hbm, kbuf.at[1], loc_s.at[1])
    lv = pltpu.make_async_copy(v_hbm, vbuf.at[1], loc_s.at[2])
    lp = pltpu.make_async_copy(kp_hbm, kpraw.at[1], loc_s.at[3])
    for cp in (lq, lk, lv, lp):
        cp.start()

    own_rows = pl.multiple_of(core * 1024 + z * 256, 256)

    def own_weight(j, which):
        src = (gate_hbm, up_hbm)[which]
        return pltpu.make_async_copy(
            src.at[:, pl.ds(j * CW, CW)],
            wbuf.at[j, pl.ds(own_rows, 256), pl.ds(which * CW, CW)],
            wl_s,
        )

    for j in range(CHUNKS):
        own_weight(j, 0).start()
        own_weight(j, 1).start()

    barrier = pltpu.get_barrier_semaphore()
    peers = 0
    for r in range(1, 8):
        pl.semaphore_signal(
            barrier, inc=1, device_id={"ctx": ctx_at(r // 4, r % 4), "tp": t}, device_id_type=MESH
        )
        pl.semaphore_signal(
            barrier, inc=1, device_id={"ctx": c, "tp": (t + r) % 8}, device_id_type=MESH
        )
        pl.semaphore_signal(
            barrier, inc=1, device_id={"ctx": across, "tp": (t + r) % 8}, device_id_type=MESH
        )
        peers += 3
    pl.semaphore_signal(barrier, inc=1, device_id={"ctx": partner, "tp": t}, device_id_type=MESH)
    pl.semaphore_wait(barrier, peers + 1)

    kv = [
        remote(k_hbm, kbuf.at[0], kv_ss.at[0], kv_rs.at[0], ctx=partner, tp=t),
        remote(v_hbm, vbuf.at[0], kv_ss.at[1], kv_rs.at[1], ctx=partner, tp=t),
        remote(kp_hbm, kpraw.at[0], kv_ss.at[2], kv_rs.at[2], ctx=partner, tp=t),
    ]

    def q_copy(r):
        return remote(
            q_hbm, q_all.at[r], q_ss, q_rs.at[r], ctx=ctx_at(r // 4, 4 - hop(r)), tp=t
        )

    kv[2].start()
    for r in (1, 2, 4):
        q_copy(r).start()
    kv[0].start()
    kv[1].start()

    def q_pass(r):
        rows = pl.ds(pl.multiple_of(64 * (r - 1), 64), 64)
        return remote(
            q_all.at[r, rows], q_all.at[3, rows], q_ss, q_rs.at[3], ctx=ctx_at(0, 5 - 2 * r), tp=t
        )

    def q_forward(r):
        return remote(q_all.at[r], q_all.at[r + 4], q_ss, q_rs.at[r + 4], ctx=across, tp=t)

    y = t // 2
    piece = pl.ds(pl.multiple_of(xh * 2048 + t * 256, 256), 256)
    far_piece = pl.ds(pl.multiple_of((1 - xh) * 2048 + t * 256, 256), 256)
    wide = pl.ds(pl.multiple_of(xh * 2048 + y * 512, 512), 512)

    lres = pltpu.make_async_copy(resid_hbm.at[:, wide], resid_own, loc_s.at[4])
    lgain = pltpu.make_async_copy(gain_hbm.at[piece], gain_buf, loc_s.at[5])
    lwide = pltpu.make_async_copy(gain_hbm.at[wide], gain_wide, loc_s.at[6])
    rres = remote(
        resid_hbm.at[:, far_piece], resid, kv_ss.at[3], kv_rs.at[3], ctx=across, tp=t
    )

    def ow_copy(s):
        return pltpu.make_async_copy(ow_hbm.at[:, pl.ds(s * 256, 256)], ow.at[s], ow_s)

    def later_loads():
        rres.start()
        lres.start()
        lgain.start()
        lwide.start()
        for s in range(16):
            ow_copy(s).start()

    def block(zz):
        return pl.multiple_of(core * 1024 + ((zz + 4) % 4) * 256, 256)

    def direct(j, way):
        rows = pl.ds(own_rows, 256)
        return remote(
            wbuf.at[j, rows],
            wbuf.at[j, rows],
            d_ss,
            d_rs.at[j],
            ctx=(up_z, down_z)[way],
            tp=t,
        )

    def direct_both(j):
        direct(j, 0).start()
        direct(j, 1).start()

    def arrived(ref, sem):
        remote(ref, ref, d_ss, sem, ctx=partner, tp=t).wait_recv()

    def left(ref, sem):
        remote(ref, ref, sem, d_rs.at[0], ctx=partner, tp=t).wait_send()

    def forward(j, way):
        at = wbuf.at[j, pl.ds(block(z - 1 if way == 0 else z + 1), 256), pl.ds(way * CW, CW)]
        return remote(at, at, f_ss, f_rs.at[j], ctx=(up_z, down_z)[way], tp=t)

    def relay(j, dz):
        at = wbuf.at[j, pl.ds(block(z + dz), 256)]
        return remote(at, at, r_ss, r_rs.at[j], ctx=partner, tp=t)

    def pass_on(j):
        arrived(wbuf.at[j, 0:512], d_rs.at[j])
        for way in (0, 1):
            forward(j, way).start()
        for dz in (0, 1, 3):
            relay(j, dz).start()

    def hand_over(j):
        arrived(wbuf.at[j, 0:256], f_rs.at[j])
        relay(j, 2).start()

    def prepare(half):
        def turn(a, _):
            rows = pl.ds(pl.multiple_of(a * 128, 128), 128)
            vt[half, :, rows] = jnp.transpose(vbuf[half, rows, :].astype(F32)).astype(BF16)
            places = jnp.broadcast_to(kpraw[half, pl.ds(a, 1), :].astype(F32), (128, 128))
            kposb[half, rows, :] = jnp.transpose(places)
            return 0

        lax.fori_loop(0, 16, turn, 0, unroll=4)

    cvec[...] = jnp.exp2(jnp.broadcast_to(exps_ref[0:1, 0:1], (8, 128)).astype(F32)) * BASE
    acc_u[...] = jnp.zeros_like(acc_u)
    acc_s[...] = jnp.zeros_like(acc_s)
    for cp in (lq, lk, lv, lp):
        cp.wait()
    prepare(1)

    def qk(i, j, buf, mref):
        r = turn_owner((i + 1) // 2)
        half = (i + 1) % 2
        owner = ctx_at(r // 4, hop(r))
        qpos = qp_ref[pl.ds(owner, 1), :].astype(F32)
        qc = jnp.concatenate([q_all[r, :, h * HD : (h + 1) * HD] for h in range(4)], axis=0)
        s = lax.dot_general(
            kbuf[half, j * KT : (j + 1) * KT], qc, NT, preferred_element_type=F32
        )
        visible = kposb[half, j * KT : (j + 1) * KT] <= qpos
        s = jnp.concatenate(
            [jnp.where(visible, s[:, h * HD : (h + 1) * HD], LOW) for h in range(4)], axis=1
        )
        buf[...] = s
        mref[...] = jnp.max(s, axis=0, keepdims=True)

    def pv(i, j, buf, mref, state):
        half = (i + 1) % 2
        factor = cvec[0:1, 0:1]
        top = jnp.maximum(state[0], mref[...])
        p = jnp.exp2((buf[...] - top) * factor)
        total = jnp.sum(p, axis=0, keepdims=True)
        out = lax.dot_general(
            vt[half, :, j * KT : (j + 1) * KT], p.astype(BF16), NN, preferred_element_type=F32
        )
        keep = jnp.exp2((state[0] - top) * factor)
        return (top, state[1] * keep + total, state[2] * keep + out)

    def u_copy(r):
        return remote(usend.at[r], urecv.at[r], u_ss, u_rs, ctx=ctx_at(0, hop(r)), tp=t)

    def s_copy(r):
        return remote(ssend.at[r], srecv.at[r], st_ss, st_rs, ctx=ctx_at(0, hop(r)), tp=t)

    def u_across(r):
        return remote(usend.at[r], uhalf.at[r - 4], u_ss, uh_rs.at[r - 4], ctx=across, tp=t)

    def s_across(r):
        return remote(ssend.at[r], shalf.at[r - 4], st_ss, sh_rs.at[r - 4], ctx=across, tp=t)

    def combine(r):
        s_across(r + 4).wait_recv()
        u_across(r + 4).wait_recv()
        factor = cvec[0:1, 0:1]
        mine, theirs = ssend[r, 0:1, :], shalf[r, 0:1, :]
        top = jnp.maximum(mine, theirs)
        keep, add = jnp.exp2((mine - top) * factor), jnp.exp2((theirs - top) * factor)
        ssend[r, 0:1, :] = top
        ssend[r, 1:2, :] = ssend[r, 1:2, :] * keep + shalf[r, 1:2, :] * add
        usend[r] = (usend[r].astype(F32) * keep + uhalf[r].astype(F32) * add).astype(BF16)
        s_copy(r).start()
        u_copy(r).start()

    mine = wbuf.at[:, pl.ds(own_rows, 256)]
    pltpu.make_async_copy(mine, mine, wl_s).wait()
    direct_both(0)
    qk(0, 0, sa, ma)
    qk(0, 1, sb, mb)
    state = (jnp.full((1, 512), LOW, F32), jnp.zeros((1, 512), F32), jnp.zeros((128, 512), F32))
    state = pv(0, 0, sa, ma, state)
    state = pv(0, 1, sb, mb, state)
    ssend[0, 0:1, :] = state[0]
    ssend[0, 1:2, :] = state[1]
    usend[0] = state[2].astype(BF16)
    for cp in kv:
        cp.wait_recv()
    prepare(0)
    for r in (1, 2):
        q_copy(r).wait_recv()
        q_pass(r).start()
        q_forward(r).start()
    direct_both(1)
    qk(1, 0, sa, ma)

    def step(i, _):
        odd = i % 2
        r = turn_owner((i + 1) // 2)
        r_next = turn_owner((i + 2) // 2)

        @pl.when((odd == 1) & (i > 10))
        def _():
            m = (i - 11) // 2
            combine(1 + 2 * m - 3 * (m // 2))

            @pl.when(i == 15)
            def _():
                pass_on(3)
                direct_both(6)

        @pl.when((odd == 0) & (i < 9))
        def _():
            direct_both(i // 2 + 1)

        @pl.when((i == 4) | (i == 6) | (i == 9))
        def _():
            pass_on(i // 3 - 1)

        pl.when(i == 7)(later_loads)

        @pl.when(i == 3)
        def _():
            q_copy(3).wait_recv()
            q_forward(3).start()

        @pl.when((odd == 0) & (i < 10))
        def _():
            q_copy(r_next).wait_recv()

        before = jnp.where(odd == 1, LOW, acc_s[0:1, :])
        state = (before, acc_s[1:2, :], acc_u[...])
        qk(i, 1, sb, mb)
        state = pv(i, 0, sa, ma, state)
        qk(i + 1, 0, sa, ma)
        state = pv(i, 1, sb, mb, state)
        acc_s[0:1, :] = state[0]
        acc_s[1:2, :] = state[1]
        acc_u[...] = state[2]

        @pl.when(odd == 0)
        def _():
            usend[r] = acc_u[...].astype(BF16)
            ssend[r] = acc_s[...]

            @pl.when((i > 2) & (i < 12))
            def _():
                s_across(r).start()
                u_across(r).start()

        return 0

    lax.fori_loop(1, 16, step, 0)

    pass_on(4)
    direct_both(7)
    pass_on(5)
    for j in (8, 9, 10):
        direct_both(j)

    arrived(srecv.at[1:4], st_rs)
    s_across(4).wait_recv()
    tops = [acc_s[0:1, :], ssend[0, 0:1, :], shalf[0, 0:1, :]] + [srecv[r, 0:1, :] for r in (1, 2, 3)]
    sums = [acc_s[1:2, :], ssend[0, 1:2, :], shalf[0, 1:2, :]] + [srecv[r, 1:2, :] for r in (1, 2, 3)]
    top = functools.reduce(jnp.maximum, tops)
    factor = cvec[0:1, 0:1]
    shares = [jnp.exp2((m - top) * factor) for m in tops]
    total = functools.reduce(jnp.add, [w * l for w, l in zip(shares, sums)])
    merged = acc_u[...] * shares[0] + usend[0].astype(F32) * shares[1]
    u_across(4).wait_recv()
    merged = merged + uhalf[0].astype(F32) * shares[2]
    arrived(urecv.at[1:4], u_rs)
    for r in (1, 2, 3):
        merged = merged + urecv[r].astype(F32) * shares[r + 2]
    value_factor = jnp.exp2(jnp.broadcast_to(exps_ref[0:1, 1:2], (8, 128)).astype(F32))[0:1, 0:1]
    merged = merged * (value_factor / total)
    attention = jnp.concatenate(
        [jnp.transpose(merged[:, h * HD : (h + 1) * HD]) for h in range(4)], axis=1
    ).astype(BF16)

    pltpu.make_async_copy(ow, ow, ow_s).wait()

    def peer(k):
        return ((y + k) % 4) * 2 + t % 2

    neighbour = y * 2 + 1 - t % 2

    def p_copy(k):
        return remote(rs_send.at[k], rs_recv.at[k], p_ss, p_rs, ctx=across, tp=(t + k) % 8)

    def w_copy(k):
        return remote(ws_send.at[k], ws_recv.at[k], w_ss, w_rs, ctx=c, tp=peer(k))

    def swap_copy():
        return remote(swap_send, swap_recv, sw_ss, sw_rs, ctx=c, tp=neighbour)

    def product(at):
        return lax.dot_general(attention, ow[at], NN, preferred_element_type=F32)

    for k in (0, 4, 3, 5, 2, 6, 1, 7):
        rs_send[k] = product((1 - xh) * 8 + (t + k) % 8).astype(BF16)
        p_copy(k).start()
    for k in (2, 1, 3):
        at = xh * 8 + ((y + k) % 4) * 2
        ws_send[k, :, 0:256] = product(at).astype(BF16)
        ws_send[k, :, 256:512] = product(at + 1).astype(BF16)
        w_copy(k).start()
    own[:, 0:256] = product(xh * 8 + y * 2)
    own[:, 256:512] = product(xh * 8 + y * 2 + 1)
    lres.wait()
    lgain.wait()
    lwide.wait()
    rres.wait_recv()

    lane = pl.ds(pl.multiple_of(y * 256, 256), 256)

    def g_cross():
        at = gbuf.at[t % 2, 1, :, lane]
        return remote(gsend, at, g_ss.at[2], g_rs.at[2], ctx=c, tp=neighbour)

    def g_copy(k):
        at = gbuf.at[t % 2, 1, :, lane]
        return remote(gsend, at, g_ss.at[1], g_rs.at[1], ctx=c, tp=peer(k))

    def g_forward(k):
        at = gbuf.at[1 - t % 2, 1, :, lane]
        return remote(at, at, g_ss.at[1], g_rs.at[1], ctx=c, tp=peer(k))

    def gw_copy(k):
        return remote(
            gsend_wide, gbuf.at[:, 0, :, lane], g_ss.at[0], g_rs.at[0], ctx=c, tp=peer(k)
        )

    def row_sums(stream):
        return lax.dot_general(
            jnp.ones((8, stream.shape[1]), F32),
            stream * stream,
            NT,
            preferred_element_type=F32,
            precision=lax.Precision.HIGHEST,
        )

    def spread_far():
        arrived(rs_recv, p_rs)
        stream = resid[...].astype(F32)
        for k in range(8):
            stream = stream + rs_recv[k].astype(F32)
        gain = jnp.broadcast_to(gain_buf[...].astype(F32).reshape(1, 256), (128, 256))
        scaled = (stream * gain).astype(BF16)
        gsend[...] = scaled
        g_cross().start()
        for k in (2, 1, 3):
            g_copy(k).start()
        gbuf[t % 2, 1, :, lane] = scaled
        far_squares[...] = row_sums(stream)
        for k in range(1, 8):
            sq_copy(k).start()

    def swap_own():
        arrived(ws_recv.at[1:4], w_rs)
        stream = own[...]
        for k in (1, 2, 3):
            stream = stream + ws_recv[k].astype(F32)
        swap_send[...] = stream.astype(BF16)
        swap_copy().start()
        own[...] = stream + resid_own[...].astype(F32)

    def spread_own():
        swap_copy().wait_recv()
        stream = own[...] + swap_recv[...].astype(F32)
        gain = jnp.broadcast_to(gain_wide[...].astype(F32).reshape(1, 512), (128, 512))
        scaled = (stream * gain).astype(BF16)
        gsend_wide[0] = scaled[:, 0:256]
        gsend_wide[1] = scaled[:, 256:512]
        for k in (2, 1, 3):
            gw_copy(k).start()
        gbuf[0, 0, :, lane] = scaled[:, 0:256]
        gbuf[1, 0, :, lane] = scaled[:, 256:512]
        own_squares[...] = row_sums(stream)
        for k in (2, 1, 3):
            oq_copy(k).start()

    def sq_copy(k):
        return remote(far_squares, sq_recv.at[k], sq_ss.at[0], sq_rs.at[0], ctx=c, tp=(t + k) % 8)

    def oq_copy(k):
        return remote(own_squares, oq_recv.at[k], sq_ss.at[1], sq_rs.at[1], ctx=c, tp=peer(k))

    def sq_swap():
        return remote(sq_recv.at[0], sq_other, sq_ss.at[2], sq_rs.at[2], ctx=across, tp=t)

    for j in (6, 7):
        pass_on(j)
        direct_both(j + 5)
    spread_far()
    g_cross().wait_recv()
    for k in (2, 1, 3):
        g_forward(k).start()
    swap_own()
    pass_on(8)
    direct_both(13)
    hand_over(0)

    def swap_squares():
        arrived(sq_recv.at[1:8], sq_rs.at[0])
        squares = far_squares[...]
        for k in range(1, 8):
            squares = squares + sq_recv[k]
        sq_recv[0] = squares
        sq_swap().start()

    def find_scale():
        sq_swap().wait_recv()
        arrived(oq_recv.at[1:4], sq_rs.at[1])
        squares = sq_other[...] + own_squares[...]
        for k in (1, 2, 3):
            squares = squares + oq_recv[k]
        scale_row = lax.rsqrt(squares[0:1, :] * (1.0 / 4096.0) + 1e-05)
        scale[...] = jnp.transpose(jnp.broadcast_to(scale_row, (128, 128)))

    def x_copy(j):
        return remote(xsend.at[j], xrecv.at[j], x_ss, x_rs.at[j], ctx=across, tp=t)

    def finish(j):
        x_copy(j).wait_recv()
        both = (pown[j] + xrecv[j].astype(F32)) * scale[:, 0:1]
        gate = both[:, :CW]
        up = both[:, CW:]
        out_ref[:, pl.ds(pl.multiple_of(j * CW, CW), CW)] = (gate / (1.0 + jnp.exp(-gate)) * up).astype(BF16)

    def half_product(j, side):
        return lax.dot_general(
            gbuf[0, side], wbuf[j, 0:1024, :], NN, preferred_element_type=F32
        ) + lax.dot_general(
            gbuf[1, side], wbuf[j, 1024:2048, :], NN, preferred_element_type=F32
        )

    def drain():
        for cp in kv:
            cp.wait_send()
        rres.wait_send()
        left(q_all.at[1:8], q_ss)
        left(usend.at[1:8], u_ss)
        left(ssend.at[1:8], st_ss)
        left(rs_send, p_ss)
        left(ws_send.at[1:4], w_ss)
        swap_copy().wait_send()
        left(ws_send.at[1:4], g_ss.at[0])
        left(rs_send.at[0:6], g_ss.at[1])
        g_cross().wait_send()
        left(sq_recv.at[1:8], sq_ss.at[0])
        left(oq_recv.at[1:4], sq_ss.at[1])
        sq_swap().wait_send()
        left(wbuf.at[:, 0:512], d_ss)
        left(wbuf.at[:, 0:256], f_ss)
        left(wbuf.at[:, 0:1024], r_ss)

    arrived(rs_recv.at[0:6], g_rs.at[1])

    def chunk(j, _):
        for j_at, j_new in ((0, 9), (2, 10), (4, 11), (6, 12), (8, 13)):

            @pl.when(j == j_at)
            def _(j_new=j_new):
                pass_on(j_new)

        pl.when(j == 4)(swap_squares)

        @pl.when(j < CHUNKS - 1)
        def _():
            hand_over(j + 1)

        arrived(wbuf.at[j, 0:1024], r_rs.at[j])
        xsend[j] = half_product(j, 1).astype(BF16)
        x_copy(j).start()

        pl.when(j == 2)(spread_own)

        @pl.when(j == LAG)
        def _():
            arrived(ws_recv.at[1:4], g_rs.at[0])

        @pl.when(j >= LAG)
        def _():
            pown[j - LAG] = half_product(j - LAG, 0)

        pl.when(j == 10)(find_scale)

        @pl.when(j >= 10)
        def _():
            finish(j - 10)

        return 0

    lax.fori_loop(0, CHUNKS, chunk, 0)
    for j in range(CHUNKS - LAG, CHUNKS):
        pown[j] = half_product(j, 0)
    for j in range(CHUNKS - 10, CHUNKS):
        finish(j)

    drain()
    left(xsend, x_ss)


def body(
    queries,
    key_cache,
    value_cache,
    scale_exps,
    query_pos,
    key_pos,
    resid,
    out_weight,
    norm_gain,
    gate_weight,
    up_weight,
):
    vmem = pl.BlockSpec(memory_space=pltpu.VMEM)
    hbm = pl.BlockSpec(memory_space=pl.ANY)
    V = pltpu.VMEM
    dma = pltpu.SemaphoreType.DMA
    return pl.pallas_call(
        kernel,
        out_shape=pltpu.VMEM((128, 1792), BF16),
        in_specs=[hbm, hbm, hbm, vmem, vmem, hbm, hbm, hbm, hbm, hbm, hbm],
        out_specs=vmem,
        scratch_shapes=[
            V((8, 128, 512), BF16),
            V((2, 2048, 128), BF16),
            V((2, 2048, 128), BF16),
            V((2, 128, 2048), BF16),
            V((2, 16, 128), jnp.int32),
            V((2, 2048, 128), F32),
            V((KT, 512), F32),
            V((KT, 512), F32),
            V((1, 512), F32),
            V((1, 512), F32),
            V((128, 512), F32),
            V((2, 512), F32),
            V((8, 128), F32),
            V((8, 128, 512), BF16),
            V((8, 2, 512), F32),
            V((4, 128, 512), BF16),
            V((4, 2, 512), F32),
            V((4, 128, 512), BF16),
            V((4, 2, 512), F32),
            V((16, 512, 256), BF16),
            V((128, 256), BF16),
            V((128, 512), BF16),
            V((256,), BF16),
            V((512,), BF16),
            V((8, 128, 256), BF16),
            V((8, 128, 256), BF16),
            V((4, 128, 512), BF16),
            V((4, 128, 512), BF16),
            V((128, 512), BF16),
            V((128, 512), BF16),
            V((128, 512), F32),
            V((8, 128), F32),
            V((8, 128), F32),
            V((8, 8, 128), F32),
            V((4, 8, 128), F32),
            V((8, 128), F32),
            V((128, 256), BF16),
            V((2, 128, 256), BF16),
            V((2, 2, 128, 1024), BF16),
            V((CHUNKS, 2048, 2 * CW), BF16),
            V((CHUNKS, 128, 2 * CW), BF16),
            V((CHUNKS, 128, 2 * CW), BF16),
            V((CHUNKS, 128, 2 * CW), F32),
            V((128, 128), F32),
            dma,
            dma((8,)),
            dma((4,)),
            dma((4,)),
            dma((7,)),
            dma,
            dma,
            dma,
            dma,
            dma,
            dma,
            dma((4,)),
            dma((4,)),
            dma,
            dma((CHUNKS,)),
            dma,
            dma((CHUNKS,)),
            dma,
            dma((CHUNKS,)),
            dma,
            dma,
            dma,
            dma,
            dma,
            dma,
            dma((3,)),
            dma((3,)),
            dma((3,)),
            dma((3,)),
            dma,
            dma((CHUNKS,)),
        ],
        compiler_params=pltpu.CompilerParams(
            collective_id=0, has_side_effects=True, vmem_limit_bytes=60 * 2**20
        ),
        cost_estimate=pl.CostEstimate(
            flops=18_000_000_000, bytes_accessed=16_000_000, transcendentals=17_000_000
        ),
    )(
        queries,
        key_cache,
        value_cache,
        scale_exps.T,
        query_pos.reshape(16, 128),
        key_pos.reshape(16, 128),
        resid,
        out_weight,
        norm_gain,
        gate_weight,
        up_weight,
    )


def solution(mesh):
    placed = (
        P("ctx", "tp"),
        P("ctx", "tp"),
        P("ctx", "tp"),
        P(None, "tp"),
        P(),
        P("ctx"),
        P("ctx", None),
        P("tp", None),
        P(),
        P("ctx", "tp"),
        P("ctx", "tp"),
    )
    return jax.shard_map(
        body, mesh=mesh, in_specs=placed, out_specs=P("ctx", "tp"), check_vma=False
    )
```

```python
import functools
import math

import jax
import jax.numpy as jnp
from jax import lax
from jax.experimental import pallas as pl
from jax.experimental.pallas import tpu as pltpu
from jax.sharding import PartitionSpec as P

HD = 128
NT = (((1,), (1,)), ((), ()))
NN = (((1,), (0,)), ((), ()))
MESH = pl.DeviceIdType.MESH
LOW = -1e30
BASE = math.log2(math.e) / math.sqrt(HD)
F32 = jnp.float32
BF16 = jnp.bfloat16
KT = 1024
CHUNKS = 14
CW = 128
LAG = 7


def hop(r):
    low = r % 4
    return ((low * (low + 1)) // 2) % 4


def turn_owner(n):
    n = n % 8
    return n + 3 * ((n + 6) // 8) - 4 * ((n + 3) // 8) - 2 * ((n + 2) // 8) - 2 * (n // 7)


def kernel(
    q_hbm,
    k_hbm,
    v_hbm,
    exps_hbm,
    qp_hbm,
    kp_hbm,
    resid_hbm,
    ow_hbm,
    gain_hbm,
    gate_hbm,
    up_hbm,
    out_ref,
    q_all,
    kbuf,
    vbuf,
    vt,
    exps_ref,
    qp_ref,
    kpraw,
    kposb,
    sa,
    sb,
    ma,
    mb,
    acc_u,
    acc_s,
    cvec,
    usend,
    ssend,
    urecv,
    srecv,
    uhalf,
    shalf,
    ow,
    resid,
    resid_own,
    gain_buf,
    gain_wide,
    rs_send,
    rs_recv,
    ws_send,
    ws_recv,
    swap_send,
    swap_recv,
    own,
    far_squares,
    own_squares,
    sq_recv,
    oq_recv,
    sq_other,
    gsend,
    gsend_wide,
    gbuf,
    wbuf,
    xsend,
    xrecv,
    pown,
    scale,
    q_ss,
    q_rs,
    kv_ss,
    kv_rs,
    loc_s,
    ow_s,
    wl_s,
    u_ss,
    u_rs,
    st_ss,
    st_rs,
    uh_rs,
    sh_rs,
    d_ss,
    d_rs,
    f_ss,
    f_rs,
    r_ss,
    r_rs,
    p_ss,
    p_rs,
    w_ss,
    w_rs,
    sw_ss,
    sw_rs,
    sq_ss,
    sq_rs,
    g_ss,
    g_rs,
    x_ss,
    x_rs,
):
    c = lax.axis_index("ctx")
    t = lax.axis_index("tp")
    core = c % 2
    z = (c // 2) % 4
    xh = c // 8

    def ctx_at(dx, dz, dc=0):
        return ((xh + dx) % 2) * 8 + ((z + dz + 4) % 4) * 2 + (core + dc) % 2

    partner = ctx_at(0, 0, 1)
    across = ctx_at(1, 0)
    up_z = ctx_at(0, 1)
    down_z = ctx_at(0, 3)

    def remote(src, dst, ss, rs, **dev):
        return pltpu.make_async_remote_copy(
            src_ref=src, dst_ref=dst, send_sem=ss, recv_sem=rs, device_id=dev, device_id_type=MESH
        )

    barrier = pltpu.get_barrier_semaphore()
    peers = 0
    for r in range(1, 8):
        pl.semaphore_signal(
            barrier, inc=1, device_id={"ctx": ctx_at(r // 4, r % 4), "tp": t}, device_id_type=MESH
        )
        pl.semaphore_signal(
            barrier, inc=1, device_id={"ctx": c, "tp": (t + r) % 8}, device_id_type=MESH
        )
        pl.semaphore_signal(
            barrier, inc=1, device_id={"ctx": across, "tp": (t + r) % 8}, device_id_type=MESH
        )
        peers += 3
    pl.semaphore_signal(barrier, inc=1, device_id={"ctx": partner, "tp": t}, device_id_type=MESH)

    lq = pltpu.make_async_copy(q_hbm, q_all.at[0], loc_s.at[0])
    lk = pltpu.make_async_copy(k_hbm, kbuf.at[1], loc_s.at[1])
    lv = pltpu.make_async_copy(v_hbm, vbuf.at[1], loc_s.at[2])
    lp = pltpu.make_async_copy(kp_hbm, kpraw.at[1], loc_s.at[3])
    lx = pltpu.make_async_copy(exps_hbm, exps_ref, loc_s.at[7])
    lt = pltpu.make_async_copy(qp_hbm, qp_ref, loc_s.at[8])
    for cp in (lq, lk, lv, lp, lx, lt):
        cp.start()

    own_rows = pl.multiple_of(core * 1024 + z * 256, 256)

    def own_weight(j, which):
        src = (gate_hbm, up_hbm)[which]
        return pltpu.make_async_copy(
            src.at[:, pl.ds(j * CW, CW)],
            wbuf.at[j, pl.ds(own_rows, 256), pl.ds(which * CW, CW)],
            wl_s,
        )

    for j in range(CHUNKS):
        own_weight(j, 0).start()
        own_weight(j, 1).start()

    pl.semaphore_wait(barrier, peers + 1)

    kv = [
        remote(kbuf.at[1], kbuf.at[0], kv_ss.at[0], kv_rs.at[0], ctx=partner, tp=t),
        remote(vbuf.at[1], vbuf.at[0], kv_ss.at[1], kv_rs.at[1], ctx=partner, tp=t),
        remote(kpraw.at[1], kpraw.at[0], kv_ss.at[2], kv_rs.at[2], ctx=partner, tp=t),
    ]

    def q_copy(r):
        return remote(
            q_all.at[0], q_all.at[r], q_ss, q_rs.at[r], ctx=ctx_at(r // 4, 4 - hop(r)), tp=t
        )

    for cp in (lq, lk, lv, lp, lx, lt):
        cp.wait()
    for r in (2, 1, 4):
        q_copy(r).start()
    for cp in kv:
        cp.start()

    def q_pass(r):
        rows = pl.ds(pl.multiple_of(64 * (r - 1), 64), 64)
        return remote(
            q_all.at[r, rows], q_all.at[3, rows], q_ss, q_rs.at[3], ctx=ctx_at(0, 5 - 2 * r), tp=t
        )

    def q_forward(r):
        return remote(q_all.at[r], q_all.at[r + 4], q_ss, q_rs.at[r + 4], ctx=across, tp=t)

    y = t // 2
    piece = pl.ds(pl.multiple_of(xh * 2048 + t * 256, 256), 256)
    far_piece = pl.ds(pl.multiple_of((1 - xh) * 2048 + t * 256, 256), 256)
    wide = pl.ds(pl.multiple_of(xh * 2048 + y * 512, 512), 512)

    lres = pltpu.make_async_copy(resid_hbm.at[:, wide], resid_own, loc_s.at[4])
    lgain = pltpu.make_async_copy(gain_hbm.at[piece], gain_buf, loc_s.at[5])
    lwide = pltpu.make_async_copy(gain_hbm.at[wide], gain_wide, loc_s.at[6])
    rres = remote(
        resid_hbm.at[:, far_piece], resid, kv_ss.at[3], kv_rs.at[3], ctx=across, tp=t
    )

    def ow_copy(s):
        return pltpu.make_async_copy(ow_hbm.at[:, pl.ds(s * 256, 256)], ow.at[s], ow_s)

    def later_loads():
        rres.start()
        lres.start()
        lgain.start()
        lwide.start()
        for s in range(16):
            ow_copy(s).start()

    def block(zz):
        return pl.multiple_of(core * 1024 + ((zz + 4) % 4) * 256, 256)

    def direct(j, way):
        rows = pl.ds(own_rows, 256)
        return remote(
            wbuf.at[j, rows],
            wbuf.at[j, rows],
            d_ss,
            d_rs.at[j],
            ctx=(up_z, down_z)[way],
            tp=t,
        )

    def direct_both(j):
        direct(j, 0).start()
        direct(j, 1).start()

    def arrived(ref, sem):
        remote(ref, ref, d_ss, sem, ctx=partner, tp=t).wait_recv()

    def left(ref, sem):
        remote(ref, ref, sem, d_rs.at[0], ctx=partner, tp=t).wait_send()

    def forward(j, way):
        at = wbuf.at[j, pl.ds(block(z - 1 if way == 0 else z + 1), 256), pl.ds(way * CW, CW)]
        return remote(at, at, f_ss, f_rs.at[j], ctx=(up_z, down_z)[way], tp=t)

    def relay(j, dz):
        at = wbuf.at[j, pl.ds(block(z + dz), 256)]
        return remote(at, at, r_ss, r_rs.at[j], ctx=partner, tp=t)

    def pass_on(j):
        arrived(wbuf.at[j, 0:512], d_rs.at[j])
        for way in (0, 1):
            forward(j, way).start()
        for dz in (0, 1, 3):
            relay(j, dz).start()

    def hand_over(j):
        arrived(wbuf.at[j, 0:256], f_rs.at[j])
        relay(j, 2).start()

    def prepare(half):
        def turn(a, _):
            rows = pl.ds(pl.multiple_of(a * 128, 128), 128)
            vt[half, :, rows] = jnp.transpose(vbuf[half, rows, :].astype(F32)).astype(BF16)
            places = jnp.broadcast_to(kpraw[half, pl.ds(a, 1), :].astype(F32), (128, 128))
            kposb[half, rows, :] = jnp.transpose(places)
            return 0

        lax.fori_loop(0, 16, turn, 0, unroll=4)

    cvec[...] = jnp.exp2(jnp.broadcast_to(exps_ref[0:1, 0:1], (8, 128)).astype(F32)) * BASE
    acc_u[...] = jnp.zeros_like(acc_u)
    acc_s[...] = jnp.zeros_like(acc_s)
    prepare(1)

    def qk(i, j, buf, mref):
        r = turn_owner((i + 1) // 2)
        half = (i + 1) % 2
        owner = ctx_at(r // 4, hop(r))
        qpos = qp_ref[pl.ds(owner, 1), :].astype(F32)
        qc = jnp.concatenate([q_all[r, :, h * HD : (h + 1) * HD] for h in range(4)], axis=0)
        s = lax.dot_general(
            kbuf[half, j * KT : (j + 1) * KT], qc, NT, preferred_element_type=F32
        )
        visible = kposb[half, j * KT : (j + 1) * KT] <= qpos
        s = jnp.concatenate(
            [jnp.where(visible, s[:, h * HD : (h + 1) * HD], LOW) for h in range(4)], axis=1
        )
        buf[...] = s
        mref[...] = jnp.max(s, axis=0, keepdims=True)

    def pv(i, j, buf, mref, state):
        half = (i + 1) % 2
        factor = cvec[0:1, 0:1]
        top = jnp.maximum(state[0], mref[...])
        p = jnp.exp2((buf[...] - top) * factor)
        total = jnp.sum(p, axis=0, keepdims=True)
        out = lax.dot_general(
            vt[half, :, j * KT : (j + 1) * KT], p.astype(BF16), NN, preferred_element_type=F32
        )
        keep = jnp.exp2((state[0] - top) * factor)
        return (top, state[1] * keep + total, state[2] * keep + out)

    def u_copy(r):
        return remote(usend.at[r], urecv.at[r], u_ss, u_rs, ctx=ctx_at(0, hop(r)), tp=t)

    def s_copy(r):
        return remote(ssend.at[r], srecv.at[r], st_ss, st_rs, ctx=ctx_at(0, hop(r)), tp=t)

    def u_across(r):
        return remote(usend.at[r], uhalf.at[r - 4], u_ss, uh_rs.at[r - 4], ctx=across, tp=t)

    def s_across(r):
        return remote(ssend.at[r], shalf.at[r - 4], st_ss, sh_rs.at[r - 4], ctx=across, tp=t)

    def combine(r):
        s_across(r + 4).wait_recv()
        u_across(r + 4).wait_recv()
        factor = cvec[0:1, 0:1]
        mine, theirs = ssend[r, 0:1, :], shalf[r, 0:1, :]
        top = jnp.maximum(mine, theirs)
        keep, add = jnp.exp2((mine - top) * factor), jnp.exp2((theirs - top) * factor)
        ssend[r, 0:1, :] = top
        ssend[r, 1:2, :] = ssend[r, 1:2, :] * keep + shalf[r, 1:2, :] * add
        usend[r] = (usend[r].astype(F32) * keep + uhalf[r].astype(F32) * add).astype(BF16)
        s_copy(r).start()
        u_copy(r).start()

    mine = wbuf.at[:, pl.ds(own_rows, 256)]
    pltpu.make_async_copy(mine, mine, wl_s).wait()
    direct_both(0)
    qk(0, 0, sa, ma)
    qk(0, 1, sb, mb)
    state = (jnp.full((1, 512), LOW, F32), jnp.zeros((1, 512), F32), jnp.zeros((128, 512), F32))
    state = pv(0, 0, sa, ma, state)
    state = pv(0, 1, sb, mb, state)
    ssend[0, 0:1, :] = state[0]
    ssend[0, 1:2, :] = state[1]
    usend[0] = state[2].astype(BF16)
    for cp in kv:
        cp.wait_recv()
    prepare(0)
    for r in (1, 2):
        q_copy(r).wait_recv()
        q_pass(r).start()
        q_forward(r).start()
    direct_both(1)
    qk(1, 0, sa, ma)

    def step(i, _):
        odd = i % 2
        r = turn_owner((i + 1) // 2)
        r_next = turn_owner((i + 2) // 2)

        @pl.when((odd == 1) & (i > 10))
        def _():
            m = (i - 11) // 2
            combine(1 + 2 * m - 3 * (m // 2))

            @pl.when(i == 15)
            def _():
                pass_on(3)
                pass_on(4)
                direct_both(6)

        @pl.when((odd == 0) & (i < 9))
        def _():
            direct_both(i // 2 + 1)

        @pl.when((i == 4) | (i == 6) | (i == 9))
        def _():
            pass_on(i // 3 - 1)

        pl.when(i == 7)(later_loads)

        @pl.when(i == 3)
        def _():
            q_copy(3).wait_recv()
            q_forward(3).start()

        @pl.when((odd == 0) & (i < 10))
        def _():
            q_copy(r_next).wait_recv()

        before = jnp.where(odd == 1, LOW, acc_s[0:1, :])
        state = (before, acc_s[1:2, :], acc_u[...])
        qk(i, 1, sb, mb)
        state = pv(i, 0, sa, ma, state)
        qk(i + 1, 0, sa, ma)
        state = pv(i, 1, sb, mb, state)
        acc_s[0:1, :] = state[0]
        acc_s[1:2, :] = state[1]
        acc_u[...] = state[2]

        @pl.when(odd == 0)
        def _():
            usend[r] = acc_u[...].astype(BF16)
            ssend[r] = acc_s[...]

            @pl.when((i > 2) & (i < 12))
            def _():
                s_across(r).start()
                u_across(r).start()

        return 0

    lax.fori_loop(1, 16, step, 0)

    direct_both(7)
    pass_on(5)
    for j in (8, 9, 10):
        direct_both(j)

    arrived(srecv.at[1:4], st_rs)
    s_across(4).wait_recv()
    tops = [acc_s[0:1, :], ssend[0, 0:1, :], shalf[0, 0:1, :]] + [srecv[r, 0:1, :] for r in (1, 2, 3)]
    sums = [acc_s[1:2, :], ssend[0, 1:2, :], shalf[0, 1:2, :]] + [srecv[r, 1:2, :] for r in (1, 2, 3)]
    top = functools.reduce(jnp.maximum, tops)
    factor = cvec[0:1, 0:1]
    shares = [jnp.exp2((m - top) * factor) for m in tops]
    total = functools.reduce(jnp.add, [w * l for w, l in zip(shares, sums)])
    merged = acc_u[...] * shares[0] + usend[0].astype(F32) * shares[1]
    u_across(4).wait_recv()
    merged = merged + uhalf[0].astype(F32) * shares[2]
    arrived(urecv.at[1:4], u_rs)
    for r in (1, 2, 3):
        merged = merged + urecv[r].astype(F32) * shares[r + 2]
    value_factor = jnp.exp2(jnp.broadcast_to(exps_ref[0:1, 1:2], (8, 128)).astype(F32))[0:1, 0:1]
    merged = merged * (value_factor / total)
    attention = jnp.concatenate(
        [jnp.transpose(merged[:, h * HD : (h + 1) * HD]) for h in range(4)], axis=1
    ).astype(BF16)

    pltpu.make_async_copy(ow, ow, ow_s).wait()

    def peer(k):
        return ((y + k) % 4) * 2 + t % 2

    neighbour = y * 2 + 1 - t % 2

    def p_copy(k):
        return remote(rs_send.at[k], rs_recv.at[k], p_ss, p_rs, ctx=across, tp=(t + k) % 8)

    def w_copy(k):
        return remote(ws_send.at[k], ws_recv.at[k], w_ss, w_rs, ctx=c, tp=peer(k))

    def swap_copy():
        return remote(swap_send, swap_recv, sw_ss, sw_rs, ctx=c, tp=neighbour)

    def product(at):
        return lax.dot_general(attention, ow[at], NN, preferred_element_type=F32)

    for k in (0, 4, 3, 5, 2, 6, 1, 7):
        rs_send[k] = product((1 - xh) * 8 + (t + k) % 8).astype(BF16)
        p_copy(k).start()
    for k in (2, 1, 3):
        at = xh * 8 + ((y + k) % 4) * 2
        ws_send[k, :, 0:256] = product(at).astype(BF16)
        ws_send[k, :, 256:512] = product(at + 1).astype(BF16)
        w_copy(k).start()
    own[:, 0:256] = product(xh * 8 + y * 2)
    own[:, 256:512] = product(xh * 8 + y * 2 + 1)
    lres.wait()
    lgain.wait()
    lwide.wait()
    rres.wait_recv()

    lane = pl.ds(pl.multiple_of(y * 256, 256), 256)

    def g_cross():
        at = gbuf.at[t % 2, 1, :, lane]
        return remote(gsend, at, g_ss.at[2], g_rs.at[2], ctx=c, tp=neighbour)

    def g_copy(k):
        at = gbuf.at[t % 2, 1, :, lane]
        return remote(gsend, at, g_ss.at[1], g_rs.at[1], ctx=c, tp=peer(k))

    def g_forward(k):
        at = gbuf.at[1 - t % 2, 1, :, lane]
        return remote(at, at, g_ss.at[1], g_rs.at[1], ctx=c, tp=peer(k))

    def gw_copy(k):
        return remote(
            gsend_wide, gbuf.at[:, 0, :, lane], g_ss.at[0], g_rs.at[0], ctx=c, tp=peer(k)
        )

    def row_sums(stream):
        return lax.dot_general(
            jnp.ones((8, stream.shape[1]), F32),
            stream * stream,
            NT,
            preferred_element_type=F32,
            precision=lax.Precision.HIGHEST,
        )

    def spread_far():
        arrived(rs_recv, p_rs)
        stream = resid[...].astype(F32)
        for k in range(8):
            stream = stream + rs_recv[k].astype(F32)
        gain = jnp.broadcast_to(gain_buf[...].astype(F32).reshape(1, 256), (128, 256))
        scaled = (stream * gain).astype(BF16)
        gsend[...] = scaled
        g_cross().start()
        for k in (2, 1, 3):
            g_copy(k).start()
        gbuf[t % 2, 1, :, lane] = scaled
        far_squares[...] = row_sums(stream)
        for k in range(1, 8):
            sq_copy(k).start()

    def swap_own():
        arrived(ws_recv.at[1:4], w_rs)
        stream = own[...]
        for k in (1, 2, 3):
            stream = stream + ws_recv[k].astype(F32)
        swap_send[...] = stream.astype(BF16)
        swap_copy().start()
        own[...] = stream + resid_own[...].astype(F32)

    def spread_own():
        swap_copy().wait_recv()
        stream = own[...] + swap_recv[...].astype(F32)
        gain = jnp.broadcast_to(gain_wide[...].astype(F32).reshape(1, 512), (128, 512))
        scaled = (stream * gain).astype(BF16)
        gsend_wide[0] = scaled[:, 0:256]
        gsend_wide[1] = scaled[:, 256:512]
        for k in (2, 1, 3):
            gw_copy(k).start()
        gbuf[0, 0, :, lane] = scaled[:, 0:256]
        gbuf[1, 0, :, lane] = scaled[:, 256:512]
        own_squares[...] = row_sums(stream)
        for k in (2, 1, 3):
            oq_copy(k).start()

    def sq_copy(k):
        return remote(far_squares, sq_recv.at[k], sq_ss.at[0], sq_rs.at[0], ctx=c, tp=(t + k) % 8)

    def oq_copy(k):
        return remote(own_squares, oq_recv.at[k], sq_ss.at[1], sq_rs.at[1], ctx=c, tp=peer(k))

    def sq_swap():
        return remote(sq_recv.at[0], sq_other, sq_ss.at[2], sq_rs.at[2], ctx=across, tp=t)

    for j in (6, 7):
        pass_on(j)
        direct_both(j + 5)
    spread_far()
    g_cross().wait_recv()
    for k in (2, 1, 3):
        g_forward(k).start()
    swap_own()
    pass_on(8)
    direct_both(13)
    hand_over(0)

    def swap_squares():
        arrived(sq_recv.at[1:8], sq_rs.at[0])
        squares = far_squares[...]
        for k in range(1, 8):
            squares = squares + sq_recv[k]
        sq_recv[0] = squares
        sq_swap().start()

    def find_scale():
        sq_swap().wait_recv()
        arrived(oq_recv.at[1:4], sq_rs.at[1])
        squares = sq_other[...] + own_squares[...]
        for k in (1, 2, 3):
            squares = squares + oq_recv[k]
        scale_row = lax.rsqrt(squares[0:1, :] * (1.0 / 4096.0) + 1e-05)
        scale[...] = jnp.transpose(jnp.broadcast_to(scale_row, (128, 128)))

    def x_copy(j):
        return remote(xsend.at[j], xrecv.at[j], x_ss, x_rs.at[j], ctx=across, tp=t)

    def finish(j):
        x_copy(j).wait_recv()
        both = (pown[j] + xrecv[j].astype(F32)) * scale[:, 0:1]
        gate = both[:, :CW]
        up = both[:, CW:]
        out_ref[:, pl.ds(pl.multiple_of(j * CW, CW), CW)] = (gate / (1.0 + jnp.exp(-gate)) * up).astype(BF16)

    def half_product(j, side):
        return lax.dot_general(
            gbuf[0, side], wbuf[j, 0:1024, :], NN, preferred_element_type=F32
        ) + lax.dot_general(
            gbuf[1, side], wbuf[j, 1024:2048, :], NN, preferred_element_type=F32
        )

    def drain():
        for cp in kv:
            cp.wait_send()
        rres.wait_send()
        left(q_all.at[1:8], q_ss)
        left(usend.at[1:8], u_ss)
        left(ssend.at[1:8], st_ss)
        left(rs_send, p_ss)
        left(ws_send.at[1:4], w_ss)
        swap_copy().wait_send()
        left(ws_send.at[1:4], g_ss.at[0])
        left(rs_send.at[0:6], g_ss.at[1])
        g_cross().wait_send()
        left(sq_recv.at[1:8], sq_ss.at[0])
        left(oq_recv.at[1:4], sq_ss.at[1])
        sq_swap().wait_send()
        left(wbuf.at[:, 0:512], d_ss)
        left(wbuf.at[:, 0:256], f_ss)
        left(wbuf.at[:, 0:1024], r_ss)

    arrived(rs_recv.at[0:6], g_rs.at[1])

    def chunk(j, _):
        for j_at, j_new in ((1, 9), (3, 10), (5, 11), (7, 12), (9, 13)):

            @pl.when(j == j_at)
            def _(j_new=j_new):
                pass_on(j_new)

        pl.when(j == 4)(swap_squares)

        @pl.when(j < CHUNKS - 1)
        def _():
            hand_over(j + 1)

        arrived(wbuf.at[j, 0:1024], r_rs.at[j])
        xsend[j] = half_product(j, 1).astype(BF16)
        x_copy(j).start()

        pl.when(j == 2)(spread_own)

        @pl.when(j == LAG)
        def _():
            arrived(ws_recv.at[1:4], g_rs.at[0])

        @pl.when(j >= LAG)
        def _():
            pown[j - LAG] = half_product(j - LAG, 0)

        pl.when(j == 10)(find_scale)

        @pl.when(j >= 10)
        def _():
            finish(j - 10)

        return 0

    lax.fori_loop(0, CHUNKS, chunk, 0)
    for j in range(CHUNKS - LAG, CHUNKS):
        pown[j] = half_product(j, 0)
    for j in range(CHUNKS - 10, CHUNKS):
        finish(j)

    drain()
    left(xsend, x_ss)


def body(
    queries,
    key_cache,
    value_cache,
    scale_exps,
    query_pos,
    key_pos,
    resid,
    out_weight,
    norm_gain,
    gate_weight,
    up_weight,
):
    vmem = pl.BlockSpec(memory_space=pltpu.VMEM)
    hbm = pl.BlockSpec(memory_space=pl.ANY)
    V = pltpu.VMEM
    dma = pltpu.SemaphoreType.DMA
    return pl.pallas_call(
        kernel,
        out_shape=pltpu.VMEM((128, 1792), BF16),
        in_specs=[hbm, hbm, hbm, hbm, hbm, hbm, hbm, hbm, hbm, hbm, hbm],
        out_specs=vmem,
        scratch_shapes=[
            V((8, 128, 512), BF16),
            V((2, 2048, 128), BF16),
            V((2, 2048, 128), BF16),
            V((2, 128, 2048), BF16),
            V((1, 2), jnp.int32),
            V((16, 128), jnp.int32),
            V((2, 16, 128), jnp.int32),
            V((2, 2048, 128), F32),
            V((KT, 512), F32),
            V((KT, 512), F32),
            V((1, 512), F32),
            V((1, 512), F32),
            V((128, 512), F32),
            V((2, 512), F32),
            V((8, 128), F32),
            V((8, 128, 512), BF16),
            V((8, 2, 512), F32),
            V((4, 128, 512), BF16),
            V((4, 2, 512), F32),
            V((4, 128, 512), BF16),
            V((4, 2, 512), F32),
            V((16, 512, 256), BF16),
            V((128, 256), BF16),
            V((128, 512), BF16),
            V((256,), BF16),
            V((512,), BF16),
            V((8, 128, 256), BF16),
            V((8, 128, 256), BF16),
            V((4, 128, 512), BF16),
            V((4, 128, 512), BF16),
            V((128, 512), BF16),
            V((128, 512), BF16),
            V((128, 512), F32),
            V((8, 128), F32),
            V((8, 128), F32),
            V((8, 8, 128), F32),
            V((4, 8, 128), F32),
            V((8, 128), F32),
            V((128, 256), BF16),
            V((2, 128, 256), BF16),
            V((2, 2, 128, 1024), BF16),
            V((CHUNKS, 2048, 2 * CW), BF16),
            V((CHUNKS, 128, 2 * CW), BF16),
            V((CHUNKS, 128, 2 * CW), BF16),
            V((CHUNKS, 128, 2 * CW), F32),
            V((128, 128), F32),
            dma,
            dma((8,)),
            dma((4,)),
            dma((4,)),
            dma((9,)),
            dma,
            dma,
            dma,
            dma,
            dma,
            dma,
            dma((4,)),
            dma((4,)),
            dma,
            dma((CHUNKS,)),
            dma,
            dma((CHUNKS,)),
            dma,
            dma((CHUNKS,)),
            dma,
            dma,
            dma,
            dma,
            dma,
            dma,
            dma((3,)),
            dma((3,)),
            dma((3,)),
            dma((3,)),
            dma,
            dma((CHUNKS,)),
        ],
        compiler_params=pltpu.CompilerParams(
            collective_id=0, has_side_effects=True, vmem_limit_bytes=60 * 2**20
        ),
        cost_estimate=pl.CostEstimate(
            flops=18_000_000_000, bytes_accessed=16_000_000, transcendentals=17_000_000
        ),
    )(
        queries,
        key_cache,
        value_cache,
        scale_exps.T,
        query_pos.reshape(16, 128),
        key_pos.reshape(16, 128),
        resid,
        out_weight,
        norm_gain,
        gate_weight,
        up_weight,
    )


def solution(mesh):
    placed = (
        P("ctx", "tp"),
        P("ctx", "tp"),
        P("ctx", "tp"),
        P(None, "tp"),
        P(),
        P("ctx"),
        P("ctx", None),
        P("tp", None),
        P(),
        P("ctx", "tp"),
        P("ctx", "tp"),
    )
    return jax.shard_map(
        body, mesh=mesh, in_specs=placed, out_specs=P("ctx", "tp"), check_vma=False
    )
```

```python
import functools
import math

import jax
import jax.numpy as jnp
from jax import lax
from jax.experimental import pallas as pl
from jax.experimental.pallas import tpu as pltpu
from jax.sharding import PartitionSpec as P

HD = 128
NT = (((1,), (1,)), ((), ()))
NN = (((1,), (0,)), ((), ()))
MESH = pl.DeviceIdType.MESH
LOW = -1e30
BASE = math.log2(math.e) / math.sqrt(HD)
F32 = jnp.float32
BF16 = jnp.bfloat16
KT = 1024
CHUNKS = 14
CW = 128
LAG = 7


def hop(r):
    low = r % 4
    return ((low * (low + 1)) // 2) % 4


def turn_owner(n):
    n = n % 8
    return n + 3 * ((n + 6) // 8) - 4 * ((n + 3) // 8) - 2 * ((n + 2) // 8) - 2 * (n // 7)


def kernel(
    q_hbm,
    k_hbm,
    v_hbm,
    exps_hbm,
    qp_hbm,
    kp_hbm,
    resid_hbm,
    ow_hbm,
    gain_hbm,
    gate_hbm,
    up_hbm,
    out_ref,
    q_all,
    kbuf,
    vbuf,
    vt,
    exps_ref,
    qp_ref,
    kpraw,
    kposb,
    sa,
    sb,
    ma,
    mb,
    acc_u,
    acc_s,
    cvec,
    usend,
    ssend,
    urecv,
    srecv,
    uhalf,
    shalf,
    ow,
    resid,
    resid_own,
    gain_buf,
    gain_wide,
    rs_send,
    rs_recv,
    ws_send,
    ws_recv,
    swap_send,
    swap_recv,
    own,
    far_squares,
    own_squares,
    sq_recv,
    oq_recv,
    sq_other,
    gsend,
    gsend_wide,
    gbuf,
    wbuf,
    xsend,
    xrecv,
    pown,
    scale,
    q_ss,
    q_rs,
    kv_ss,
    kv_rs,
    loc_s,
    ow_s,
    wl_s,
    u_ss,
    u_rs,
    st_ss,
    st_rs,
    uh_rs,
    sh_rs,
    d_ss,
    d_rs,
    f_ss,
    f_rs,
    r_ss,
    r_rs,
    p_ss,
    p_rs,
    w_ss,
    w_rs,
    sw_ss,
    sw_rs,
    sq_ss,
    sq_rs,
    g_ss,
    g_rs,
    x_ss,
    x_rs,
):
    c = lax.axis_index("ctx")
    t = lax.axis_index("tp")
    core = c % 2
    z = (c // 2) % 4
    xh = c // 8

    def ctx_at(dx, dz, dc=0):
        return ((xh + dx) % 2) * 8 + ((z + dz + 4) % 4) * 2 + (core + dc) % 2

    partner = ctx_at(0, 0, 1)
    across = ctx_at(1, 0)
    up_z = ctx_at(0, 1)
    down_z = ctx_at(0, 3)

    def remote(src, dst, ss, rs, **dev):
        return pltpu.make_async_remote_copy(
            src_ref=src, dst_ref=dst, send_sem=ss, recv_sem=rs, device_id=dev, device_id_type=MESH
        )

    barrier = pltpu.get_barrier_semaphore()
    peers = 0
    for r in range(1, 8):
        pl.semaphore_signal(
            barrier, inc=1, device_id={"ctx": ctx_at(r // 4, r % 4), "tp": t}, device_id_type=MESH
        )
        pl.semaphore_signal(
            barrier, inc=1, device_id={"ctx": c, "tp": (t + r) % 8}, device_id_type=MESH
        )
        pl.semaphore_signal(
            barrier, inc=1, device_id={"ctx": across, "tp": (t + r) % 8}, device_id_type=MESH
        )
        peers += 3
    pl.semaphore_signal(barrier, inc=1, device_id={"ctx": partner, "tp": t}, device_id_type=MESH)

    lq = pltpu.make_async_copy(q_hbm, q_all.at[0], loc_s.at[0])
    lk = pltpu.make_async_copy(k_hbm, kbuf.at[1], loc_s.at[1])
    lv = pltpu.make_async_copy(v_hbm, vbuf.at[1], loc_s.at[2])
    lp = pltpu.make_async_copy(kp_hbm, kpraw.at[1], loc_s.at[3])
    lx = pltpu.make_async_copy(exps_hbm, exps_ref, loc_s.at[7])
    lt = pltpu.make_async_copy(qp_hbm, qp_ref, loc_s.at[8])
    for cp in (lq, lk, lv, lp, lx, lt):
        cp.start()

    own_rows = pl.multiple_of(core * 1024 + z * 256, 256)

    def own_weight(j, which):
        src = (gate_hbm, up_hbm)[which]
        return pltpu.make_async_copy(
            src.at[:, pl.ds(j * CW, CW)],
            wbuf.at[j, pl.ds(own_rows, 256), pl.ds(which * CW, CW)],
            wl_s,
        )

    for j in range(CHUNKS):
        own_weight(j, 0).start()
        own_weight(j, 1).start()

    pl.semaphore_wait(barrier, peers + 1)

    kv = [
        remote(kbuf.at[1], kbuf.at[0], kv_ss.at[0], kv_rs.at[0], ctx=partner, tp=t),
        remote(vbuf.at[1], vbuf.at[0], kv_ss.at[1], kv_rs.at[1], ctx=partner, tp=t),
        remote(kpraw.at[1], kpraw.at[0], kv_ss.at[2], kv_rs.at[2], ctx=partner, tp=t),
    ]

    def q_copy(r):
        return remote(
            q_all.at[0], q_all.at[r], q_ss, q_rs.at[r], ctx=ctx_at(r // 4, 4 - hop(r)), tp=t
        )

    for cp in (lq, lk, lv, lp, lx, lt):
        cp.wait()
    for r in (2, 1, 4):
        q_copy(r).start()
    for cp in kv:
        cp.start()

    def q_pass(r):
        rows = pl.ds(pl.multiple_of(64 * (r - 1), 64), 64)
        return remote(
            q_all.at[r, rows], q_all.at[3, rows], q_ss, q_rs.at[3], ctx=ctx_at(0, 5 - 2 * r), tp=t
        )

    def q_forward(r):
        return remote(q_all.at[r], q_all.at[r + 4], q_ss, q_rs.at[r + 4], ctx=across, tp=t)

    y = t // 2
    piece = pl.ds(pl.multiple_of(xh * 2048 + t * 256, 256), 256)
    far_piece = pl.ds(pl.multiple_of((1 - xh) * 2048 + t * 256, 256), 256)
    wide = pl.ds(pl.multiple_of(xh * 2048 + y * 512, 512), 512)

    lres = pltpu.make_async_copy(resid_hbm.at[:, wide], resid_own, loc_s.at[4])
    lgain = pltpu.make_async_copy(gain_hbm.at[piece], gain_buf, loc_s.at[5])
    lwide = pltpu.make_async_copy(gain_hbm.at[wide], gain_wide, loc_s.at[6])
    rres = remote(
        resid_hbm.at[:, far_piece], resid, kv_ss.at[3], kv_rs.at[3], ctx=across, tp=t
    )

    def ow_copy(s):
        return pltpu.make_async_copy(ow_hbm.at[:, pl.ds(s * 256, 256)], ow.at[s], ow_s)

    def later_loads():
        rres.start()
        lres.start()
        lgain.start()
        lwide.start()
        for s in range(16):
            ow_copy(s).start()

    def block(zz):
        return pl.multiple_of(core * 1024 + ((zz + 4) % 4) * 256, 256)

    def direct(j, way):
        rows = pl.ds(own_rows, 256)
        return remote(
            wbuf.at[j, rows],
            wbuf.at[j, rows],
            d_ss,
            d_rs.at[j],
            ctx=(up_z, down_z)[way],
            tp=t,
        )

    def direct_both(j):
        direct(j, 0).start()
        direct(j, 1).start()

    def arrived(ref, sem):
        remote(ref, ref, d_ss, sem, ctx=partner, tp=t).wait_recv()

    def left(ref, sem):
        remote(ref, ref, sem, d_rs.at[0], ctx=partner, tp=t).wait_send()

    def forward(j, way):
        at = wbuf.at[j, pl.ds(block(z - 1 if way == 0 else z + 1), 256), pl.ds(way * CW, CW)]
        return remote(at, at, f_ss, f_rs.at[j], ctx=(up_z, down_z)[way], tp=t)

    def relay(j, dz):
        at = wbuf.at[j, pl.ds(block(z + dz), 256)]
        return remote(at, at, r_ss, r_rs.at[j], ctx=partner, tp=t)

    def pass_on(j):
        arrived(wbuf.at[j, 0:512], d_rs.at[j])
        for way in (0, 1):
            forward(j, way).start()
        for dz in (0, 1, 3):
            relay(j, dz).start()

    def hand_over(j):
        arrived(wbuf.at[j, 0:256], f_rs.at[j])
        relay(j, 2).start()

    def prepare(half):
        def turn(a, _):
            rows = pl.ds(pl.multiple_of(a * 128, 128), 128)
            vt[half, :, rows] = jnp.transpose(vbuf[half, rows, :].astype(F32)).astype(BF16)
            places = jnp.broadcast_to(kpraw[half, pl.ds(a, 1), :].astype(F32), (128, 128))
            kposb[half, rows, :] = jnp.transpose(places)
            return 0

        lax.fori_loop(0, 16, turn, 0, unroll=4)

    cvec[...] = jnp.exp2(jnp.broadcast_to(exps_ref[0:1, 0:1], (8, 128)).astype(F32)) * BASE
    acc_u[...] = jnp.zeros_like(acc_u)
    acc_s[...] = jnp.zeros_like(acc_s)
    prepare(1)

    def qk(i, j, buf, mref):
        r = turn_owner((i + 1) // 2)
        half = (i + 1) % 2
        owner = ctx_at(r // 4, hop(r))
        qpos = qp_ref[pl.ds(owner, 1), :].astype(F32)
        qc = jnp.concatenate([q_all[r, :, h * HD : (h + 1) * HD] for h in range(4)], axis=0)
        s = lax.dot_general(
            kbuf[half, j * KT : (j + 1) * KT], qc, NT, preferred_element_type=F32
        )
        visible = kposb[half, j * KT : (j + 1) * KT] <= qpos
        s = jnp.concatenate(
            [jnp.where(visible, s[:, h * HD : (h + 1) * HD], LOW) for h in range(4)], axis=1
        )
        buf[...] = s
        mref[...] = jnp.max(s, axis=0, keepdims=True)

    def pv(i, j, buf, mref, state):
        half = (i + 1) % 2
        factor = cvec[0:1, 0:1]
        top = jnp.maximum(state[0], mref[...])
        p = jnp.exp2((buf[...] - top) * factor)
        total = jnp.sum(p, axis=0, keepdims=True)
        out = lax.dot_general(
            vt[half, :, j * KT : (j + 1) * KT], p.astype(BF16), NN, preferred_element_type=F32
        )
        keep = jnp.exp2((state[0] - top) * factor)
        return (top, state[1] * keep + total, state[2] * keep + out)

    def u_copy(r):
        return remote(usend.at[r], urecv.at[r], u_ss, u_rs, ctx=ctx_at(0, hop(r)), tp=t)

    def s_copy(r):
        return remote(ssend.at[r], srecv.at[r], st_ss, st_rs, ctx=ctx_at(0, hop(r)), tp=t)

    def u_across(r):
        return remote(usend.at[r], uhalf.at[r - 4], u_ss, uh_rs.at[r - 4], ctx=across, tp=t)

    def s_across(r):
        return remote(ssend.at[r], shalf.at[r - 4], st_ss, sh_rs.at[r - 4], ctx=across, tp=t)

    def combine(r):
        s_across(r + 4).wait_recv()
        u_across(r + 4).wait_recv()
        factor = cvec[0:1, 0:1]
        mine, theirs = ssend[r, 0:1, :], shalf[r, 0:1, :]
        top = jnp.maximum(mine, theirs)
        keep, add = jnp.exp2((mine - top) * factor), jnp.exp2((theirs - top) * factor)
        ssend[r, 0:1, :] = top
        ssend[r, 1:2, :] = ssend[r, 1:2, :] * keep + shalf[r, 1:2, :] * add
        usend[r] = (usend[r].astype(F32) * keep + uhalf[r].astype(F32) * add).astype(BF16)
        s_copy(r).start()
        u_copy(r).start()

    mine = wbuf.at[:, pl.ds(own_rows, 256)]
    pltpu.make_async_copy(mine, mine, wl_s).wait()
    direct_both(0)
    qk(0, 0, sa, ma)
    qk(0, 1, sb, mb)
    state = (jnp.full((1, 512), LOW, F32), jnp.zeros((1, 512), F32), jnp.zeros((128, 512), F32))
    state = pv(0, 0, sa, ma, state)
    state = pv(0, 1, sb, mb, state)
    ssend[0, 0:1, :] = state[0]
    ssend[0, 1:2, :] = state[1]
    usend[0] = state[2].astype(BF16)
    for cp in kv:
        cp.wait_recv()
    prepare(0)
    for r in (1, 2):
        q_copy(r).wait_recv()
        q_pass(r).start()
        q_forward(r).start()
    direct_both(1)
    qk(1, 0, sa, ma)

    def step(i, _):
        odd = i % 2
        r = turn_owner((i + 1) // 2)
        r_next = turn_owner((i + 2) // 2)

        @pl.when((odd == 1) & (i > 10))
        def _():
            m = (i - 11) // 2
            combine(1 + 2 * m - 3 * (m // 2))

            @pl.when(i == 15)
            def _():
                pass_on(3)
                pass_on(4)
                direct_both(6)

        @pl.when((odd == 0) & (i < 9))
        def _():
            direct_both(i // 2 + 1)

        @pl.when((i == 5) | (i == 7) | (i == 10))
        def _():
            pass_on((i - 4) // 2 - i // 10)

        pl.when(i == 7)(later_loads)

        @pl.when(i == 3)
        def _():
            q_copy(3).wait_recv()
            q_forward(3).start()

        @pl.when((odd == 0) & (i < 10))
        def _():
            q_copy(r_next).wait_recv()

        before = jnp.where(odd == 1, LOW, acc_s[0:1, :])
        state = (before, acc_s[1:2, :], acc_u[...])
        qk(i, 1, sb, mb)
        state = pv(i, 0, sa, ma, state)
        qk(i + 1, 0, sa, ma)
        state = pv(i, 1, sb, mb, state)
        acc_s[0:1, :] = state[0]
        acc_s[1:2, :] = state[1]
        acc_u[...] = state[2]

        @pl.when(odd == 0)
        def _():
            usend[r] = acc_u[...].astype(BF16)
            ssend[r] = acc_s[...]

            @pl.when((i > 2) & (i < 12))
            def _():
                s_across(r).start()
                u_across(r).start()

        return 0

    lax.fori_loop(1, 16, step, 0)

    direct_both(7)
    pass_on(5)
    for j in (8, 9, 10):
        direct_both(j)

    arrived(srecv.at[1:4], st_rs)
    s_across(4).wait_recv()
    tops = [acc_s[0:1, :], ssend[0, 0:1, :], shalf[0, 0:1, :]] + [srecv[r, 0:1, :] for r in (1, 2, 3)]
    sums = [acc_s[1:2, :], ssend[0, 1:2, :], shalf[0, 1:2, :]] + [srecv[r, 1:2, :] for r in (1, 2, 3)]
    top = functools.reduce(jnp.maximum, tops)
    factor = cvec[0:1, 0:1]
    shares = [jnp.exp2((m - top) * factor) for m in tops]
    total = functools.reduce(jnp.add, [w * l for w, l in zip(shares, sums)])
    merged = acc_u[...] * shares[0] + usend[0].astype(F32) * shares[1]
    u_across(4).wait_recv()
    merged = merged + uhalf[0].astype(F32) * shares[2]
    arrived(urecv.at[1:4], u_rs)
    for r in (1, 2, 3):
        merged = merged + urecv[r].astype(F32) * shares[r + 2]
    value_factor = jnp.exp2(jnp.broadcast_to(exps_ref[0:1, 1:2], (8, 128)).astype(F32))[0:1, 0:1]
    merged = merged * (value_factor / total)
    attention = jnp.concatenate(
        [jnp.transpose(merged[:, h * HD : (h + 1) * HD]) for h in range(4)], axis=1
    ).astype(BF16)

    pltpu.make_async_copy(ow, ow, ow_s).wait()

    def peer(k):
        return ((y + k) % 4) * 2 + t % 2

    neighbour = y * 2 + 1 - t % 2

    def p_copy(k):
        return remote(rs_send.at[k], rs_recv.at[k], p_ss, p_rs, ctx=across, tp=(t + k) % 8)

    def w_copy(k):
        return remote(ws_send.at[k], ws_recv.at[k], w_ss, w_rs, ctx=c, tp=peer(k))

    def swap_copy():
        return remote(swap_send, swap_recv, sw_ss, sw_rs, ctx=c, tp=neighbour)

    def product(at):
        return lax.dot_general(attention, ow[at], NN, preferred_element_type=F32)

    for k in (0, 4, 3, 5, 2, 6, 1, 7):
        rs_send[k] = product((1 - xh) * 8 + (t + k) % 8).astype(BF16)
        p_copy(k).start()
    for k in (2, 1, 3):
        at = xh * 8 + ((y + k) % 4) * 2
        ws_send[k, :, 0:256] = product(at).astype(BF16)
        ws_send[k, :, 256:512] = product(at + 1).astype(BF16)
        w_copy(k).start()
    own[:, 0:256] = product(xh * 8 + y * 2)
    own[:, 256:512] = product(xh * 8 + y * 2 + 1)
    lres.wait()
    lgain.wait()
    lwide.wait()
    rres.wait_recv()

    lane = pl.ds(pl.multiple_of(y * 256, 256), 256)

    def g_cross():
        at = gbuf.at[t % 2, 1, :, lane]
        return remote(gsend, at, g_ss.at[2], g_rs.at[2], ctx=c, tp=neighbour)

    def g_copy(k):
        at = gbuf.at[t % 2, 1, :, lane]
        return remote(gsend, at, g_ss.at[1], g_rs.at[1], ctx=c, tp=peer(k))

    def g_forward(k):
        at = gbuf.at[1 - t % 2, 1, :, lane]
        return remote(at, at, g_ss.at[1], g_rs.at[1], ctx=c, tp=peer(k))

    def gw_copy(k):
        return remote(
            gsend_wide, gbuf.at[:, 0, :, lane], g_ss.at[0], g_rs.at[0], ctx=c, tp=peer(k)
        )

    def row_sums(stream):
        return lax.dot_general(
            jnp.ones((8, stream.shape[1]), F32),
            stream * stream,
            NT,
            preferred_element_type=F32,
            precision=lax.Precision.HIGHEST,
        )

    def spread_far():
        arrived(rs_recv, p_rs)
        stream = resid[...].astype(F32)
        for k in range(8):
            stream = stream + rs_recv[k].astype(F32)
        gain = jnp.broadcast_to(gain_buf[...].astype(F32).reshape(1, 256), (128, 256))
        scaled = (stream * gain).astype(BF16)
        gsend[...] = scaled
        g_cross().start()
        for k in (2, 1, 3):
            g_copy(k).start()
        gbuf[t % 2, 1, :, lane] = scaled
        far_squares[...] = row_sums(stream)
        for k in range(1, 8):
            sq_copy(k).start()

    def swap_own():
        arrived(ws_recv.at[1:4], w_rs)
        stream = own[...]
        for k in (1, 2, 3):
            stream = stream + ws_recv[k].astype(F32)
        swap_send[...] = stream.astype(BF16)
        swap_copy().start()
        own[...] = stream + resid_own[...].astype(F32)

    def spread_own():
        swap_copy().wait_recv()
        stream = own[...] + swap_recv[...].astype(F32)
        gain = jnp.broadcast_to(gain_wide[...].astype(F32).reshape(1, 512), (128, 512))
        scaled = (stream * gain).astype(BF16)
        gsend_wide[0] = scaled[:, 0:256]
        gsend_wide[1] = scaled[:, 256:512]
        for k in (2, 1, 3):
            gw_copy(k).start()
        gbuf[0, 0, :, lane] = scaled[:, 0:256]
        gbuf[1, 0, :, lane] = scaled[:, 256:512]
        own_squares[...] = row_sums(stream)
        for k in (2, 1, 3):
            oq_copy(k).start()

    def sq_copy(k):
        return remote(far_squares, sq_recv.at[k], sq_ss.at[0], sq_rs.at[0], ctx=c, tp=(t + k) % 8)

    def oq_copy(k):
        return remote(own_squares, oq_recv.at[k], sq_ss.at[1], sq_rs.at[1], ctx=c, tp=peer(k))

    def sq_swap():
        return remote(sq_recv.at[0], sq_other, sq_ss.at[2], sq_rs.at[2], ctx=across, tp=t)

    for j in (6, 7):
        pass_on(j)
        direct_both(j + 5)
    spread_far()
    g_cross().wait_recv()
    for k in (2, 1, 3):
        g_forward(k).start()
    swap_own()
    pass_on(8)
    direct_both(13)
    hand_over(0)

    def swap_squares():
        arrived(sq_recv.at[1:8], sq_rs.at[0])
        squares = far_squares[...]
        for k in range(1, 8):
            squares = squares + sq_recv[k]
        sq_recv[0] = squares
        sq_swap().start()

    def find_scale():
        sq_swap().wait_recv()
        arrived(oq_recv.at[1:4], sq_rs.at[1])
        squares = sq_other[...] + own_squares[...]
        for k in (1, 2, 3):
            squares = squares + oq_recv[k]
        scale_row = lax.rsqrt(squares[0:1, :] * (1.0 / 4096.0) + 1e-05)
        scale[...] = jnp.transpose(jnp.broadcast_to(scale_row, (128, 128)))

    def x_copy(j):
        return remote(xsend.at[j], xrecv.at[j], x_ss, x_rs.at[j], ctx=across, tp=t)

    def finish(j):
        x_copy(j).wait_recv()
        both = (pown[j] + xrecv[j].astype(F32)) * scale[:, 0:1]
        gate = both[:, :CW]
        up = both[:, CW:]
        out_ref[:, pl.ds(pl.multiple_of(j * CW, CW), CW)] = (gate / (1.0 + jnp.exp(-gate)) * up).astype(BF16)

    def half_product(j, side):
        return lax.dot_general(
            gbuf[0, side], wbuf[j, 0:1024, :], NN, preferred_element_type=F32
        ) + lax.dot_general(
            gbuf[1, side], wbuf[j, 1024:2048, :], NN, preferred_element_type=F32
        )

    def drain():
        for cp in kv:
            cp.wait_send()
        rres.wait_send()
        left(q_all.at[1:8], q_ss)
        left(usend.at[1:8], u_ss)
        left(ssend.at[1:8], st_ss)
        left(rs_send, p_ss)
        left(ws_send.at[1:4], w_ss)
        swap_copy().wait_send()
        left(ws_send.at[1:4], g_ss.at[0])
        left(rs_send.at[0:6], g_ss.at[1])
        g_cross().wait_send()
        left(sq_recv.at[1:8], sq_ss.at[0])
        left(oq_recv.at[1:4], sq_ss.at[1])
        sq_swap().wait_send()
        left(wbuf.at[:, 0:512], d_ss)
        left(wbuf.at[:, 0:256], f_ss)
        left(wbuf.at[:, 0:1024], r_ss)

    arrived(rs_recv.at[0:6], g_rs.at[1])

    def chunk(j, _):
        for j_at, j_new in ((1, 9), (3, 10), (5, 11), (7, 12), (9, 13)):

            @pl.when(j == j_at)
            def _(j_new=j_new):
                pass_on(j_new)

        pl.when(j == 4)(swap_squares)

        @pl.when(j < CHUNKS - 1)
        def _():
            hand_over(j + 1)

        arrived(wbuf.at[j, 0:1024], r_rs.at[j])
        xsend[j] = half_product(j, 1).astype(BF16)
        x_copy(j).start()

        pl.when(j == 2)(spread_own)

        @pl.when(j == LAG)
        def _():
            arrived(ws_recv.at[1:4], g_rs.at[0])

        @pl.when(j >= LAG)
        def _():
            pown[j - LAG] = half_product(j - LAG, 0)

        pl.when(j == 10)(find_scale)

        @pl.when(j >= 10)
        def _():
            finish(j - 10)

        return 0

    lax.fori_loop(0, CHUNKS, chunk, 0)
    for j in range(CHUNKS - LAG, CHUNKS):
        pown[j] = half_product(j, 0)
    for j in range(CHUNKS - 10, CHUNKS):
        finish(j)

    drain()
    left(xsend, x_ss)


def body(
    queries,
    key_cache,
    value_cache,
    scale_exps,
    query_pos,
    key_pos,
    resid,
    out_weight,
    norm_gain,
    gate_weight,
    up_weight,
):
    vmem = pl.BlockSpec(memory_space=pltpu.VMEM)
    hbm = pl.BlockSpec(memory_space=pl.ANY)
    V = pltpu.VMEM
    dma = pltpu.SemaphoreType.DMA
    return pl.pallas_call(
        kernel,
        out_shape=pltpu.VMEM((128, 1792), BF16),
        in_specs=[hbm, hbm, hbm, hbm, hbm, hbm, hbm, hbm, hbm, hbm, hbm],
        out_specs=vmem,
        scratch_shapes=[
            V((8, 128, 512), BF16),
            V((2, 2048, 128), BF16),
            V((2, 2048, 128), BF16),
            V((2, 128, 2048), BF16),
            V((1, 2), jnp.int32),
            V((16, 128), jnp.int32),
            V((2, 16, 128), jnp.int32),
            V((2, 2048, 128), F32),
            V((KT, 512), F32),
            V((KT, 512), F32),
            V((1, 512), F32),
            V((1, 512), F32),
            V((128, 512), F32),
            V((2, 512), F32),
            V((8, 128), F32),
            V((8, 128, 512), BF16),
            V((8, 2, 512), F32),
            V((4, 128, 512), BF16),
            V((4, 2, 512), F32),
            V((4, 128, 512), BF16),
            V((4, 2, 512), F32),
            V((16, 512, 256), BF16),
            V((128, 256), BF16),
            V((128, 512), BF16),
            V((256,), BF16),
            V((512,), BF16),
            V((8, 128, 256), BF16),
            V((8, 128, 256), BF16),
            V((4, 128, 512), BF16),
            V((4, 128, 512), BF16),
            V((128, 512), BF16),
            V((128, 512), BF16),
            V((128, 512), F32),
            V((8, 128), F32),
            V((8, 128), F32),
            V((8, 8, 128), F32),
            V((4, 8, 128), F32),
            V((8, 128), F32),
            V((128, 256), BF16),
            V((2, 128, 256), BF16),
            V((2, 2, 128, 1024), BF16),
            V((CHUNKS, 2048, 2 * CW), BF16),
            V((CHUNKS, 128, 2 * CW), BF16),
            V((CHUNKS, 128, 2 * CW), BF16),
            V((CHUNKS, 128, 2 * CW), F32),
            V((128, 128), F32),
            dma,
            dma((8,)),
            dma((4,)),
            dma((4,)),
            dma((9,)),
            dma,
            dma,
            dma,
            dma,
            dma,
            dma,
            dma((4,)),
            dma((4,)),
            dma,
            dma((CHUNKS,)),
            dma,
            dma((CHUNKS,)),
            dma,
            dma((CHUNKS,)),
            dma,
            dma,
            dma,
            dma,
            dma,
            dma,
            dma((3,)),
            dma((3,)),
            dma((3,)),
            dma((3,)),
            dma,
            dma((CHUNKS,)),
        ],
        compiler_params=pltpu.CompilerParams(
            collective_id=0, has_side_effects=True, vmem_limit_bytes=60 * 2**20
        ),
        cost_estimate=pl.CostEstimate(
            flops=18_000_000_000, bytes_accessed=16_000_000, transcendentals=17_000_000
        ),
    )(
        queries,
        key_cache,
        value_cache,
        scale_exps.T,
        query_pos.reshape(16, 128),
        key_pos.reshape(16, 128),
        resid,
        out_weight,
        norm_gain,
        gate_weight,
        up_weight,
    )


def solution(mesh):
    placed = (
        P("ctx", "tp"),
        P("ctx", "tp"),
        P("ctx", "tp"),
        P(None, "tp"),
        P(),
        P("ctx"),
        P("ctx", None),
        P("tp", None),
        P(),
        P("ctx", "tp"),
        P("ctx", "tp"),
    )
    return jax.shard_map(
        body, mesh=mesh, in_specs=placed, out_specs=P("ctx", "tp"), check_vma=False
    )
```
